1024 devices in a mesh: row: 32 (over y_hi, x, core), col: 32 (over y_lo, z).
Axes of the slice: x: 8, y: 8 (y_hi: 2, y_lo: 4; y = y_hi * 4 + y_lo), z: 8, core: 2. Of those that a mesh axis runs over, the one named last changes fastest.
Arguments:
- source_emb: float32 [32, 32, 128, 400], P('row', 'col'), may hold values from -6 to 6
- source_acc: float32 [32, 32, 128], P('row', 'col'), may hold values from 1e-05 to 0.01
- target_emb: float32 [32, 32, 128, 400], P('row', 'col'), may hold values from -7.5 to 7.5
- target_acc: float32 [32, 32, 128], P('row', 'col'), may hold values from 1e-05 to 0.01
- relations: bfloat16 [4131, 400], replicated, may hold values from -0.59765625 to 0.59765625
- src_index: int32 [32, 32, 2, 128], P('row', 'col'), may hold values from 0 to 127
- dst_index: int32 [32, 32, 2, 128], P('row', 'col'), may hold values from 0 to 127
- rel_index: int32 [32, 32, 2, 128], P('row', 'col'), may hold values from 0 to 4130
- neg_index: int32 [32, 32, 2, 1024], P('row', 'col'), may hold values from 0 to 127
Outputs:
- source_out: float32 [32, 32, 128, 400], P('row', 'col')
- source_acc_out: float32 [32, 32, 128], P('row', 'col')
- target_out: float32 [32, 32, 128, 400], P('row', 'col')
- target_acc_out: float32 [32, 32, 128], P('row', 'col')
The draws below stay inside these ranges and needn't reach their ends.
All inputs are finite; a program needn't handle non-finite values.
Results may differ from the reference program's by a relative error of at most 0.00072.
Values sent between devices are 32-bit elements; how exact they have to be, the bound alone decides.
No kernel may reach another device: no remote copies, remote signals or barrier semaphores. Data moves between devices by JAX's collectives and lax.ppermute only.
A program may use at most 32 MiB of HBM per device.

```python
import math
from functools import partial
import jax
import jax.numpy as jnp
from jax import lax

D = 400
REL = 4131
NEG = 1024
STEPS = 2
BLK = 128
GROUP = 128
N_ROW = 32
N_COL = 32


def draw_target_emb(key, part):
    key = jax.random.fold_in(key, 11)
    key_common = jax.random.fold_in(key, 1)
    key_factor = jax.random.fold_in(key, 2)
    key_rough = jax.random.fold_in(key, 3)
    common = jnp.clip(jax.random.normal(key_common, (N_ROW, N_COL, 1, D), jnp.float32), -3.0, 3.0)
    rough_part = jnp.clip(jax.random.normal(key_rough, (N_ROW, N_COL, BLK, D), jnp.float32), -3.0, 3.0)
    factor = jax.random.uniform(key_factor, (N_ROW, N_COL, BLK, 1), jnp.float32, 0.5, 1.5)
    return (common * factor + rough_part).astype(jnp.float32)


def touch_ends(entries, stream_key, smallest, high):
    spot = [jax.random.randint(jax.random.fold_in(stream_key, axis), (), 0, length) for axis, length in enumerate(entries.shape)]
    longest = entries.shape.index(max(entries.shape))
    next_to = spot[:longest] + [(spot[longest] + 1) % entries.shape[longest]] + spot[longest + 1:]
    return entries.at[tuple(spot)].set(smallest).at[tuple(next_to)].set(high)


def level_of(rng, extent, pieces, smallest, top_value):
    def one(axis_at, shards_of):
        draws = jax.random.uniform(jax.random.fold_in(jax.random.fold_in(rng, 6), axis_at), (shards_of,), jnp.float32, smallest / len(pieces), top_value / len(pieces))
        return jnp.repeat(jnp.exp(draws), extent[axis_at] // shards_of).reshape((-1,) + (1,) * (len(extent) - axis_at - 1))

    level = one(*pieces[0])
    for cut in pieces[1:]:
        level = level * one(*cut)
    return level


def noise(key, extent, scale, bound, shards=(), dtype=jnp.bfloat16):
    factor_of = level_of(key, extent, shards, -0.22, 0.18) if shards else 1.0
    result = jax.random.normal(key, extent, jnp.float32) * scale * factor_of
    return jnp.minimum(jnp.maximum(result, -bound), bound).astype(dtype)


def setup_inputs(seed: int = 0) -> dict:
    streams_of = jax.random.split(jax.random.key(seed), 10)
    return {
        "source_emb": noise(streams_of[0], (N_ROW, N_COL, BLK, D), 1.0, 6.0, ((0, 32), (1, 32)), jnp.float32),
        "source_acc": jnp.clip(jnp.exp(math.log(0.01) - 6.9077553 * jax.random.uniform(streams_of[1], (N_ROW, N_COL, BLK), jnp.float32) ** level_of(streams_of[1], (N_ROW, N_COL, BLK), ((0, 32), (1, 32)), -0.2, 0.2)), 9.999999747378752e-06, 0.01),
        "target_emb": draw_target_emb(jax.random.fold_in(streams_of[9], 71), 0),
        "target_acc": jnp.clip(jnp.exp(math.log(0.01) - 6.9077553 * jax.random.uniform(streams_of[3], (N_ROW, N_COL, BLK), jnp.float32) ** level_of(streams_of[3], (N_ROW, N_COL, BLK), ((0, 32), (1, 32)), -0.2, 0.2)), 9.999999747378752e-06, 0.01),
        "relations": noise(streams_of[4], (REL, D), 0.15, 0.59765625),
        "src_index": touch_ends(jax.random.randint(streams_of[5], (N_ROW, N_COL, STEPS, GROUP), 0, BLK), jax.random.fold_in(streams_of[5], 1), 0, BLK - 1).astype(jnp.int32),
        "dst_index": touch_ends(jax.random.randint(streams_of[6], (N_ROW, N_COL, STEPS, GROUP), 0, BLK), jax.random.fold_in(streams_of[6], 1), 0, BLK - 1).astype(jnp.int32),
        "rel_index": touch_ends(jax.random.randint(streams_of[7], (N_ROW, N_COL, STEPS, GROUP), 0, REL), jax.random.fold_in(streams_of[7], 1), 0, REL - 1).astype(jnp.int32),
        "neg_index": touch_ends(jax.random.randint(streams_of[8], (N_ROW, N_COL, STEPS, NEG), 0, BLK), jax.random.fold_in(streams_of[8], 1), 0, BLK - 1).astype(jnp.int32),
    }


learning_rate = 0.1

def complex_query(entity_rows, operator_rows):
    half_width = entity_rows.shape[1] // 2
    real_part = entity_rows[:, :half_width]
    imag_part = entity_rows[:, half_width:]
    op_real = operator_rows[:, :half_width]
    op_imag = operator_rows[:, half_width:]
    return jnp.concatenate([real_part * op_real - imag_part * op_imag, real_part * op_imag + imag_part * op_real], axis=1)

def query_back(grad_rows, operator_rows):
    half_width = grad_rows.shape[1] // 2
    grad_real = grad_rows[:, :half_width]
    grad_imag = grad_rows[:, half_width:]
    op_real = operator_rows[:, :half_width]
    op_imag = operator_rows[:, half_width:]
    return jnp.concatenate([grad_real * op_real + grad_imag * op_imag, grad_imag * op_real - grad_real * op_imag], axis=1)

def adagrad(table, sums, gradient):
    new_sums = sums + lax.optimization_barrier(jnp.mean(gradient * gradient, axis=1))
    return (table - learning_rate * gradient / jnp.sqrt(new_sums)[:, None], new_sums)

def train_bucket(relations, source, source_sums, target, target_sums, src_rows, dst_rows, rel_ids, neg_rows):
    operator_rows = relations[rel_ids].astype(jnp.float32)
    queries = complex_query(source[src_rows], operator_rows)
    matched = target[dst_rows]
    positive = lax.optimization_barrier(jnp.sum(queries * matched, axis=1))
    pos_grad = -jax.nn.sigmoid(-positive)
    queries_b = queries.astype(jnp.bfloat16)
    negatives_b = target[neg_rows].astype(jnp.bfloat16)
    scores = jnp.dot(queries_b, negatives_b.T, preferred_element_type=jnp.float32)
    weights = (jax.nn.sigmoid(scores) / NEG).astype(jnp.bfloat16)
    grad_query = pos_grad[:, None] * matched + jnp.dot(weights, negatives_b, preferred_element_type=jnp.float32)
    grad_negs = jnp.dot(weights.T, queries_b, preferred_element_type=jnp.float32)
    source_grad = jnp.zeros_like(source).at[src_rows].add(query_back(grad_query, operator_rows))
    target_grad = jnp.zeros_like(target).at[dst_rows].add(pos_grad[:, None] * queries).at[neg_rows].add(grad_negs)
    source, source_sums = adagrad(source, source_sums, source_grad)
    target, target_sums = adagrad(target, target_sums, target_grad)
    return (source, source_sums, target, target_sums)

def reference(source_emb, source_acc, target_emb, target_acc, relations, src_index, dst_index, rel_index, neg_index):
    row_step = jax.vmap(partial(train_bucket, relations))

    def one_row(row_items):
        return row_step(*row_items)
    source, source_sums, target, target_sums = (source_emb, source_acc, target_emb, target_acc)
    for rotation in range(STEPS):
        source, source_sums, target, target_sums = lax.map(one_row, (source, source_sums, target, target_sums, src_index[:, :, rotation], dst_index[:, :, rotation], rel_index[:, :, rotation], neg_index[:, :, rotation]))
        source = jnp.roll(source, 1, axis=0)
        source_sums = jnp.roll(source_sums, 1, axis=0)
        target = jnp.roll(target, 1, axis=1)
        target_sums = jnp.roll(target_sums, 1, axis=1)
    return (source, source_sums, target, target_sums)
```

```python
import functools

import jax
import jax.numpy as jnp
from jax import lax
from jax.experimental import pallas as pl
from jax.experimental.pallas import tpu as pltpu
from jax.sharding import PartitionSpec as P


learning_rate = 0.1
bf16 = jnp.bfloat16
f32 = jnp.float32
PAD = 8
CHUNK = 512

plain = (((1,), (0,)), ((), ()))
left_t = (((0,), (0,)), ((), ()))
right_t = (((1,), (1,)), ((), ()))


def mm(a, b, dims=plain):
    return lax.dot_general(a, b, dims, preferred_element_type=f32)


def two_parts(x):
    hi = x.astype(bf16)
    lo = (x - hi.astype(f32)).astype(bf16)
    return hi, lo


def one_hot(index_row, size):
    at = lax.broadcasted_iota(jnp.int32, (size, index_row.shape[1]), 0)
    return jnp.where(at == index_row, 1.0, 0.0).astype(f32)


def bucket_step(src, src_sums, tgt, tgt_sums, operators, src_rows, dst_rows, neg_rows):
    width, entities = src.shape
    half = width // 2
    negs = neg_rows.shape[1]
    lanes = 128

    pick_s = one_hot(src_rows, entities).astype(bf16)
    pick_d = one_hot(dst_rows, entities).astype(bf16)
    pick_s2 = jnp.concatenate([pick_s, pick_s], axis=0)
    pick_d2 = jnp.concatenate([pick_d, pick_d], axis=0)
    held = one_hot(neg_rows[:, :lanes], entities)
    for k in range(lanes, negs, lanes):
        held = held + one_hot(neg_rows[:, k : k + lanes], entities)
    count_col = jnp.sum(held, axis=1, keepdims=True)
    count_row = mm(jnp.ones((8, lanes), bf16), held.astype(bf16), right_t)[0:1]

    op_re, op_im = operators[:half], operators[half:]
    rows = mm(jnp.concatenate(two_parts(src), axis=1), pick_s2)
    matched = mm(jnp.concatenate(two_parts(tgt), axis=1), pick_d2)
    re, im = rows[:half], rows[half:]
    queries = jnp.concatenate([re * op_re - im * op_im, re * op_im + im * op_re], axis=0)
    positive = jnp.sum(queries * matched, axis=0, keepdims=True)
    pos_grad = -1.0 / (1.0 + jnp.exp(positive))

    queries_b = queries.astype(bf16)
    target_b = tgt.astype(bf16)
    scores = mm(target_b, queries_b, left_t)
    weights = ((1.0 / (1.0 + jnp.exp(-scores))) * (1.0 / negs)).astype(bf16)
    counted = jnp.concatenate(two_parts(weights.astype(f32) * count_col), axis=0)

    pull = mm(jnp.concatenate([target_b, target_b], axis=1), counted)
    grad = pos_grad * matched + pull
    g_re, g_im = grad[:half], grad[half:]
    back = jnp.concatenate([g_re * op_re + g_im * op_im, g_im * op_re - g_re * op_im], axis=0)
    src_grad = mm(
        jnp.concatenate(two_parts(back), axis=1), jnp.concatenate([pick_s, pick_s], axis=1), right_t
    )

    tgt_grad = mm(queries_b, weights, right_t) * count_row + mm(
        jnp.concatenate(two_parts(pos_grad * queries), axis=1),
        jnp.concatenate([pick_d, pick_d], axis=1),
        right_t,
    )

    def adagrad(table, sums, g):
        new_sums = sums + jnp.sum(g * g, axis=0, keepdims=True) * (1.0 / width)
        return table - g * (learning_rate / jnp.sqrt(new_sums)), new_sums

    src, src_sums = adagrad(src, src_sums, src_grad)
    tgt, tgt_sums = adagrad(tgt, tgt_sums, tgt_grad)
    return src, src_sums, tgt, tgt_sums


def store_block(ref, table, sums):
    width = table.shape[0]
    ref[:width, :] = table
    ref[width:, :] = jnp.broadcast_to(sums, (ref.shape[0] - width, sums.shape[1]))


def first_kernel(
    src_ref, src_sums_ref, tgt_ref, tgt_sums_ref, table_ref, s_ref, d_ref, g_ref, n_ref,
    src_out, tgt_out, op_out, table_v, pick_v, sems,
):
    width = src_ref.shape[0]
    types = table_ref.shape[1]
    cut = (width // 2 + 15) // 16 * 16
    parts = [(0, cut), (cut, width - cut)]
    copies = [
        pltpu.make_async_copy(table_ref.at[pl.ds(a, n)], table_v.at[pl.ds(a, n)], sems.at[i])
        for i, (a, n) in enumerate(parts)
    ]
    for copy in copies:
        copy.start()
    wanted = jnp.concatenate([g_ref[0, 0, 0:1, :], g_ref[0, 0, 1:2, :]], axis=1)
    for k in range(0, types, CHUNK):
        n = min(CHUNK, types - k)
        pick_v[k : k + n, :] = one_hot(wanted - k, n).astype(bf16)
    pieces = []
    for copy, (a, n) in zip(copies, parts):
        copy.wait()
        pieces.append(mm(table_v[a : a + n, :], pick_v[...]))
    operators = jnp.concatenate(pieces, axis=0)
    entities = src_ref.shape[1]
    op_out[...] = operators[:, entities:]
    src, src_sums, tgt, tgt_sums = bucket_step(
        src_ref[...], src_sums_ref[0], tgt_ref[...], tgt_sums_ref[0], operators[:, :entities],
        s_ref[0, 0, 0:1, :], d_ref[0, 0, 0:1, :], n_ref[0, 0, 0:1, :],
    )
    store_block(src_out, src, src_sums)
    store_block(tgt_out, tgt, tgt_sums)


def second_kernel(src_ref, tgt_ref, op_ref, s_ref, d_ref, n_ref, src_out, tgt_out):
    width = op_ref.shape[0]
    src, src_sums, tgt, tgt_sums = bucket_step(
        src_ref[:width, :], src_ref[width : width + 1, :], tgt_ref[:width, :], tgt_ref[width : width + 1, :],
        op_ref[...],
        s_ref[0, 0, 1:2, :], d_ref[0, 0, 1:2, :], n_ref[0, 0, 1:2, :],
    )
    store_block(src_out, src, src_sums)
    store_block(tgt_out, tgt, tgt_sums)


def shift(x, axis):
    length = lax.axis_size(axis)
    return lax.ppermute(x, axis, [(i, (i + 1) % length) for i in range(length)])


def on_device(
    source_emb, source_acc, target_emb, target_acc, relations, src_index, dst_index, rel_index, neg_index
):
    src, tgt = source_emb[0, 0].T, target_emb[0, 0].T
    width, entities = src.shape
    types = relations.shape[0]
    block = jax.ShapeDtypeStruct((width + PAD, entities), f32)
    vmem = pl.BlockSpec(memory_space=pltpu.VMEM)
    params = pltpu.CompilerParams(vmem_limit_bytes=40 * 1024 * 1024)

    src, tgt, operators = pl.pallas_call(
        first_kernel,
        name="first_step",
        out_shape=(block, block, jax.ShapeDtypeStruct((width, entities), f32)),
        in_specs=[vmem] * 4 + [pl.BlockSpec(memory_space=pl.ANY)] + [vmem] * 4,
        out_specs=(vmem, vmem, vmem),
        scratch_shapes=[
            pltpu.VMEM((width, types), bf16),
            pltpu.VMEM((types, 2 * entities), bf16),
            pltpu.SemaphoreType.DMA((2,)),
        ],
        compiler_params=params,
    )(src, source_acc, tgt, target_acc, relations.T, src_index, dst_index, rel_index, neg_index)
    src = shift(src, "row")
    tgt = shift(tgt, "col")
    src, tgt = pl.pallas_call(
        second_kernel,
        name="second_step",
        out_shape=(block, block),
        in_specs=[vmem] * 6,
        out_specs=(vmem, vmem),
        compiler_params=params,
    )(src, tgt, operators, src_index, dst_index, neg_index)
    src = shift(src, "row")
    tgt = shift(tgt, "col")
    return (
        src[:width].T[None, None],
        src[width][None, None],
        tgt[:width].T[None, None],
        tgt[width][None, None],
    )


def solution(mesh):
    grid4 = P("row", "col", None, None)
    grid3 = P("row", "col", None)
    return jax.shard_map(
        on_device,
        mesh=mesh,
        in_specs=(grid4, grid3, grid4, grid3, P(), grid4, grid4, grid4, grid4),
        out_specs=(grid4, grid3, grid4, grid3),
        check_vma=False,
    )
```

```python
import functools

import jax
import jax.numpy as jnp
from jax import lax
from jax.experimental import pallas as pl
from jax.experimental.pallas import tpu as pltpu
from jax.sharding import PartitionSpec as P


learning_rate = 0.1
bf16 = jnp.bfloat16
f32 = jnp.float32
PAD = 8
CHUNK = 512
VMEM_LIMIT = 32 * 1024 * 1024

plain = (((1,), (0,)), ((), ()))
left_t = (((0,), (0,)), ((), ()))
right_t = (((1,), (1,)), ((), ()))


def mm(a, b, dims=plain):
    return lax.dot_general(a, b, dims, preferred_element_type=f32)


def two_parts(x):
    hi = x.astype(bf16)
    lo = (x - hi.astype(f32)).astype(bf16)
    return hi, lo


def one_hot(index_row, size):
    at = lax.broadcasted_iota(jnp.int32, (size, index_row.shape[1]), 0)
    return jnp.where(at == index_row, 1.0, 0.0).astype(f32)


def bucket_step(src, src_sums, tgt, tgt_sums, operators, src_rows, dst_rows, neg_rows):
    width, entities = src.shape
    half = width // 2
    lanes = src_rows.shape[1]
    negs = lanes * len(neg_rows)

    pick_s = one_hot(src_rows, entities).astype(bf16)
    pick_d = one_hot(dst_rows, entities).astype(bf16)
    pick_s2 = jnp.concatenate([pick_s, pick_s], axis=0)
    pick_d2 = jnp.concatenate([pick_d, pick_d], axis=0)
    held = one_hot(neg_rows[0], entities)
    for row in neg_rows[1:]:
        held = held + one_hot(row, entities)
    count_col = jnp.sum(held, axis=1, keepdims=True)
    count_row = mm(jnp.ones((8, lanes), bf16), held.astype(bf16), right_t)[0:1]

    op_re, op_im = operators[:half], operators[half:]
    rows = mm(jnp.concatenate(two_parts(src), axis=1), pick_s2)
    matched = mm(jnp.concatenate(two_parts(tgt), axis=1), pick_d2)
    re, im = rows[:half], rows[half:]
    queries = jnp.concatenate([re * op_re - im * op_im, re * op_im + im * op_re], axis=0)
    positive = jnp.sum(queries * matched, axis=0, keepdims=True)
    pos_grad = -1.0 / (1.0 + jnp.exp(positive))

    queries_b = queries.astype(bf16)
    target_b = tgt.astype(bf16)
    scores = mm(target_b, queries_b, left_t)
    weights = ((1.0 / (1.0 + jnp.exp(-scores))) * (1.0 / negs)).astype(bf16)
    counted = jnp.concatenate(two_parts(weights.astype(f32) * count_col), axis=0)

    pull = mm(jnp.concatenate([target_b, target_b], axis=1), counted)
    grad = pos_grad * matched + pull
    g_re, g_im = grad[:half], grad[half:]
    back = jnp.concatenate([g_re * op_re + g_im * op_im, g_im * op_re - g_re * op_im], axis=0)
    src_grad = mm(
        jnp.concatenate(two_parts(back), axis=1), jnp.concatenate([pick_s, pick_s], axis=1), right_t
    )

    tgt_grad = mm(queries_b, weights, right_t) * count_row + mm(
        jnp.concatenate(two_parts(pos_grad * queries), axis=1),
        jnp.concatenate([pick_d, pick_d], axis=1),
        right_t,
    )

    def adagrad(table, sums, g):
        new_sums = sums + jnp.sum(g * g, axis=0, keepdims=True) * (1.0 / width)
        return table - g * (learning_rate / jnp.sqrt(new_sums)), new_sums

    src, src_sums = adagrad(src, src_sums, src_grad)
    tgt, tgt_sums = adagrad(tgt, tgt_sums, tgt_grad)
    return src, src_sums, tgt, tgt_sums


def store_block(ref, table, sums):
    width = table.shape[0]
    ref[:width, :] = table
    ref[width:, :] = jnp.broadcast_to(sums, (ref.shape[0] - width, sums.shape[1]))


def first_kernel(
    src_hbm, src_sums_hbm, tgt_hbm, tgt_sums_hbm, table_hbm, s_hbm, d_hbm, g_hbm, n_hbm,
    tgt_out, src_out, op_out, index_out,
    src_ref, src_sums_ref, tgt_ref, tgt_sums_ref, table_ref, s_ref, d_ref, g_ref, n_ref, pick_ref, sems,
):
    width, entities = src_ref.shape
    types = table_ref.shape[1]
    lanes = s_ref.shape[3]
    cut = (width // 2 + 15) // 16 * 16
    parts = [(0, cut), (cut, width - cut)]
    pairs = [(g_hbm, g_ref)]
    pairs += [(table_hbm.at[pl.ds(a, n)], table_ref.at[pl.ds(a, n)]) for a, n in parts]
    pairs += [
        (src_hbm, src_ref), (tgt_hbm, tgt_ref), (s_hbm, s_ref), (d_hbm, d_ref), (n_hbm, n_ref),
        (src_sums_hbm, src_sums_ref), (tgt_sums_hbm, tgt_sums_ref),
    ]
    copies = [pltpu.make_async_copy(a, b, sems.at[i]) for i, (a, b) in enumerate(pairs)]
    for copy in copies:
        copy.start()
    copies[0].wait()
    wanted = jnp.concatenate([g_ref[0, 0, 0:1, :], g_ref[0, 0, 1:2, :]], axis=1)
    for k in range(0, types, CHUNK):
        n = min(CHUNK, types - k)
        pick_ref[k : k + n, :] = one_hot(wanted - k, n).astype(bf16)
    pieces = []
    for copy, (a, n) in zip(copies[1:3], parts):
        copy.wait()
        pieces.append(mm(table_ref[a : a + n, :], pick_ref[...]))
    for copy in copies[3:]:
        copy.wait()
    operators = jnp.concatenate(pieces, axis=0)
    op_out[...] = operators[:, lanes:]
    index_out[0:1, :] = s_ref[0, 0, 1:2, :]
    index_out[1:2, :] = d_ref[0, 0, 1:2, :]
    for k in range(n_ref.shape[3] // lanes):
        index_out[2 + k : 3 + k, :] = n_ref[0, 0, 1:2, k * lanes : (k + 1) * lanes]
    negs = [n_ref[0, 0, 0:1, k * lanes : (k + 1) * lanes] for k in range(n_ref.shape[3] // lanes)]
    src, src_sums, tgt, tgt_sums = bucket_step(
        src_ref[...], src_sums_ref[0], tgt_ref[...], tgt_sums_ref[0], operators[:, :lanes],
        s_ref[0, 0, 0:1, :], d_ref[0, 0, 0:1, :], negs,
    )
    store_block(src_out, src, src_sums)
    store_block(tgt_out, tgt, tgt_sums)


def second_kernel(tgt_ref, src_ref, op_ref, index_ref, tgt_out, src_out):
    width = op_ref.shape[0]
    negs = [index_ref[k : k + 1, :] for k in range(2, index_ref.shape[0])]
    src, src_sums, tgt, tgt_sums = bucket_step(
        src_ref[:width, :], src_ref[width : width + 1, :], tgt_ref[:width, :], tgt_ref[width : width + 1, :],
        op_ref[...], index_ref[0:1, :], index_ref[1:2, :], negs,
    )
    store_block(src_out, src, src_sums)
    store_block(tgt_out, tgt, tgt_sums)


def unpack_kernel(tgt_ref, src_ref, src_out, src_sums_out, tgt_out, tgt_sums_out, sems):
    width = src_out.shape[0]
    pairs = []
    for ref, out, sums_out in ((src_ref, src_out, src_sums_out), (tgt_ref, tgt_out, tgt_sums_out)):
        pairs += [(ref.at[pl.ds(0, width)], out), (ref.at[pl.ds(width, 1)], sums_out.at[0])]
    copies = [pltpu.make_async_copy(a, b, sems.at[i]) for i, (a, b) in enumerate(pairs)]
    for copy in copies:
        copy.start()
    for copy in copies:
        copy.wait()


def shift(x, axis):
    length = lax.axis_size(axis)
    return lax.ppermute(x, axis, [(i, (i + 1) % length) for i in range(length)])


def on_device(
    source_emb, source_acc, target_emb, target_acc, relations, src_index, dst_index, rel_index, neg_index
):
    src, tgt = source_emb[0, 0].T, target_emb[0, 0].T
    width, entities = src.shape
    types = relations.shape[0]
    edges, negs = src_index.shape[3], neg_index.shape[3]
    block = pltpu.VMEM((width + PAD, entities), f32)
    vmem = pl.BlockSpec(memory_space=pltpu.VMEM)
    hbm = pl.BlockSpec(memory_space=pltpu.HBM)
    params = pltpu.CompilerParams(vmem_limit_bytes=VMEM_LIMIT)

    operands = (src, source_acc, tgt, target_acc, relations.T, src_index, dst_index, rel_index, neg_index)
    tgt, src, operators, index = pl.pallas_call(
        first_kernel,
        name="first_step",
        out_shape=(
            block,
            block,
            pltpu.VMEM((width, edges), f32),
            pltpu.VMEM((2 + negs // edges, edges), jnp.int32),
        ),
        in_specs=[hbm] * len(operands),
        out_specs=(vmem,) * 4,
        scratch_shapes=[pltpu.VMEM(x.shape, x.dtype) for x in operands]
        + [pltpu.VMEM((types, 2 * edges), bf16), pltpu.SemaphoreType.DMA((len(operands) + 1,))],
        compiler_params=params,
    )(*[pltpu.with_memory_space_constraint(x, pltpu.HBM) for x in operands])
    tgt = shift(tgt, "col")
    src = shift(src, "row")
    tgt, src = pl.pallas_call(
        second_kernel,
        name="second_step",
        out_shape=(block, block),
        in_specs=[vmem] * 4,
        out_specs=(vmem, vmem),
        compiler_params=params,
    )(tgt, src, operators, index)
    tgt = shift(tgt, "col")
    src = shift(src, "row")
    table = pltpu.HBM((width, entities), f32)
    sums = pltpu.HBM((1, 1, entities), f32)
    src, src_sums, tgt, tgt_sums = pl.pallas_call(
        unpack_kernel,
        name="unpack",
        out_shape=(table, sums, table, sums),
        in_specs=[vmem] * 2,
        out_specs=(hbm,) * 4,
        scratch_shapes=[pltpu.SemaphoreType.DMA((4,))],
        compiler_params=params,
    )(tgt, src)
    return src.T[None, None], src_sums, tgt.T[None, None], tgt_sums


def solution(mesh):
    grid4 = P("row", "col", None, None)
    grid3 = P("row", "col", None)
    return jax.shard_map(
        on_device,
        mesh=mesh,
        in_specs=(grid4, grid3, grid4, grid3, P(), grid4, grid4, grid4, grid4),
        out_specs=(grid4, grid3, grid4, grid3),
        check_vma=False,
    )
```

```python
import functools

import jax
import jax.numpy as jnp
from jax import lax
from jax.experimental import pallas as pl
from jax.experimental.pallas import tpu as pltpu
from jax.sharding import PartitionSpec as P


learning_rate = 0.1
bf16 = jnp.bfloat16
f32 = jnp.float32
PAD = 8
CHUNK = 512
FINAL_COST = 50
VMEM_LIMIT = 32 * 1024 * 1024

plain = (((1,), (0,)), ((), ()))
left_t = (((0,), (0,)), ((), ()))
right_t = (((1,), (1,)), ((), ()))


def cost(microseconds):
    return pl.CostEstimate(flops=int(microseconds * 1e9), bytes_accessed=0, transcendentals=0)


def mm(a, b, dims=plain):
    return lax.dot_general(a, b, dims, preferred_element_type=f32)


def two_parts(x):
    hi = x.astype(bf16)
    lo = (x - hi.astype(f32)).astype(bf16)
    return hi, lo


def one_hot(index_row, size):
    at = lax.broadcasted_iota(jnp.int32, (size, index_row.shape[1]), 0)
    return jnp.where(at == index_row, 1.0, 0.0).astype(f32)


def bucket_step(src, src_sums, tgt, tgt_sums, operators, src_rows, dst_rows, neg_rows):
    width, entities = src.shape
    half = width // 2
    lanes = src_rows.shape[1]
    negs = lanes * len(neg_rows)

    pick_s = one_hot(src_rows, entities).astype(bf16)
    pick_d = one_hot(dst_rows, entities).astype(bf16)
    pick_s2 = jnp.concatenate([pick_s, pick_s], axis=0)
    pick_d2 = jnp.concatenate([pick_d, pick_d], axis=0)
    held = one_hot(neg_rows[0], entities)
    for row in neg_rows[1:]:
        held = held + one_hot(row, entities)
    count_col = jnp.sum(held, axis=1, keepdims=True)
    count_row = mm(jnp.ones((8, lanes), bf16), held.astype(bf16), right_t)[0:1]

    op_re, op_im = operators[:half], operators[half:]
    rows = mm(jnp.concatenate(two_parts(src), axis=1), pick_s2)
    matched = mm(jnp.concatenate(two_parts(tgt), axis=1), pick_d2)
    re, im = rows[:half], rows[half:]
    queries = jnp.concatenate([re * op_re - im * op_im, re * op_im + im * op_re], axis=0)
    positive = jnp.sum(queries * matched, axis=0, keepdims=True)
    pos_grad = -1.0 / (1.0 + jnp.exp(positive))

    queries_b = queries.astype(bf16)
    target_b = tgt.astype(bf16)
    scores = mm(target_b, queries_b, left_t)
    weights = ((1.0 / (1.0 + jnp.exp(-scores))) * (1.0 / negs)).astype(bf16)
    counted = jnp.concatenate(two_parts(weights.astype(f32) * count_col), axis=0)

    pull = mm(jnp.concatenate([target_b, target_b], axis=1), counted)
    grad = pos_grad * matched + pull
    g_re, g_im = grad[:half], grad[half:]
    back = jnp.concatenate([g_re * op_re + g_im * op_im, g_im * op_re - g_re * op_im], axis=0)
    src_grad = mm(
        jnp.concatenate(two_parts(back), axis=1), jnp.concatenate([pick_s, pick_s], axis=1), right_t
    )

    tgt_grad = mm(queries_b, weights, right_t) * count_row + mm(
        jnp.concatenate(two_parts(pos_grad * queries), axis=1),
        jnp.concatenate([pick_d, pick_d], axis=1),
        right_t,
    )

    def adagrad(table, sums, g):
        new_sums = sums + jnp.sum(g * g, axis=0, keepdims=True) * (1.0 / width)
        return table - g * (learning_rate / jnp.sqrt(new_sums)), new_sums

    src, src_sums = adagrad(src, src_sums, src_grad)
    tgt, tgt_sums = adagrad(tgt, tgt_sums, tgt_grad)
    return src, src_sums, tgt, tgt_sums


def store_block(ref, table, sums):
    width = table.shape[0]
    ref[:width, :] = table
    ref[width:, :] = jnp.broadcast_to(sums, (ref.shape[0] - width, sums.shape[1]))


def crosses(row, rows):
    return lax.rem(row + 1, rows // 2) == 0


def follows_cross(row, rows):
    return lax.rem(row, rows // 2) == 0


def early_first_kernel(*refs):
    rows = lax.axis_size("row")
    pl.when(crosses(lax.axis_index("row"), rows))(lambda: first_kernel(*refs))


def late_first_kernel(done_tgt, done_op, done_index, *refs):
    rows = lax.axis_size("row")
    early = crosses(lax.axis_index("row"), rows)
    pl.when(jnp.logical_not(early))(lambda: first_kernel(*refs))

    @pl.when(early)
    def _():
        tgt_out, _, op_out, index_out = refs[9:13]
        tgt_out[...] = done_tgt[...]
        op_out[...] = done_op[...]
        index_out[...] = done_index[...]


def arrived_kernel(_, tgt_ref, out):
    out[...] = tgt_ref[: out.shape[0], :]


def early_second_kernel(_, __, *refs):
    rows = lax.axis_size("row")
    pl.when(jnp.logical_not(follows_cross(lax.axis_index("row"), rows)))(lambda: second_kernel(*refs))


def late_second_kernel(done_tgt, done_src, *refs):
    rows = lax.axis_size("row")
    late = follows_cross(lax.axis_index("row"), rows)
    pl.when(late)(lambda: second_kernel(*refs))

    @pl.when(jnp.logical_not(late))
    def _():
        tgt_out, src_out = refs[-2:]
        tgt_out[...] = done_tgt[...]
        src_out[...] = done_src[...]


def first_kernel(
    src_hbm, src_sums_hbm, tgt_hbm, tgt_sums_hbm, table_hbm, s_hbm, d_hbm, g_hbm, n_hbm,
    tgt_out, src_out, op_out, index_out,
    src_ref, src_sums_ref, tgt_ref, tgt_sums_ref, table_ref, s_ref, d_ref, g_ref, n_ref, pick_ref, sems,
):
    width, entities = src_ref.shape
    types = table_ref.shape[1]
    lanes = s_ref.shape[3]
    cut = (width // 2 + 15) // 16 * 16
    parts = [(0, cut), (cut, width - cut)]
    pairs = [(g_hbm, g_ref)]
    pairs += [(table_hbm.at[pl.ds(a, n)], table_ref.at[pl.ds(a, n)]) for a, n in parts]
    pairs += [
        (src_hbm, src_ref), (tgt_hbm, tgt_ref), (s_hbm, s_ref), (d_hbm, d_ref), (n_hbm, n_ref),
        (src_sums_hbm, src_sums_ref), (tgt_sums_hbm, tgt_sums_ref),
    ]
    copies = [pltpu.make_async_copy(a, b, sems.at[i]) for i, (a, b) in enumerate(pairs)]
    for copy in copies:
        copy.start()
    copies[0].wait()
    wanted = jnp.concatenate([g_ref[0, 0, 0:1, :], g_ref[0, 0, 1:2, :]], axis=1)
    for k in range(0, types, CHUNK):
        n = min(CHUNK, types - k)
        pick_ref[k : k + n, :] = one_hot(wanted - k, n).astype(bf16)
    pieces = []
    for copy, (a, n) in zip(copies[1:3], parts):
        copy.wait()
        pieces.append(mm(table_ref[a : a + n, :], pick_ref[...]))
    for copy in copies[3:]:
        copy.wait()
    operators = jnp.concatenate(pieces, axis=0)
    op_out[...] = operators[:, lanes:]
    index_out[0:1, :] = s_ref[0, 0, 1:2, :]
    index_out[1:2, :] = d_ref[0, 0, 1:2, :]
    for k in range(n_ref.shape[3] // lanes):
        index_out[2 + k : 3 + k, :] = n_ref[0, 0, 1:2, k * lanes : (k + 1) * lanes]
    negs = [n_ref[0, 0, 0:1, k * lanes : (k + 1) * lanes] for k in range(n_ref.shape[3] // lanes)]
    src, src_sums, tgt, tgt_sums = bucket_step(
        src_ref[...], src_sums_ref[0], tgt_ref[...], tgt_sums_ref[0], operators[:, :lanes],
        s_ref[0, 0, 0:1, :], d_ref[0, 0, 0:1, :], negs,
    )
    store_block(src_out, src, src_sums)
    store_block(tgt_out, tgt, tgt_sums)


def second_kernel(tgt_ref, src_ref, op_ref, index_ref, tgt_out, src_out):
    width = op_ref.shape[0]
    negs = [index_ref[k : k + 1, :] for k in range(2, index_ref.shape[0])]
    src, src_sums, tgt, tgt_sums = bucket_step(
        src_ref[:width, :], src_ref[width : width + 1, :], tgt_ref[:width, :], tgt_ref[width : width + 1, :],
        op_ref[...], index_ref[0:1, :], index_ref[1:2, :], negs,
    )
    store_block(src_out, src, src_sums)
    store_block(tgt_out, tgt, tgt_sums)


def unpack(ref, out, sums_out, sems):
    width = out.shape[0]
    pairs = [(ref.at[pl.ds(0, width)], out), (ref.at[pl.ds(width, 1)], sums_out.at[0])]
    copies = [pltpu.make_async_copy(a, b, sems.at[i]) for i, (a, b) in enumerate(pairs)]
    for copy in copies:
        copy.start()
    for copy in copies:
        copy.wait()


def unpack_far_kernel(far_ref, out, sums_out, sems):
    far = follows_cross(lax.axis_index("row"), lax.axis_size("row"))
    pl.when(far)(lambda: unpack(far_ref, out, sums_out, sems))


def unpack_kernel(_, __, tgt_ref, src_ref, out, sums_out, tgt_out, tgt_sums_out, sems, src_sems):
    near = jnp.logical_not(follows_cross(lax.axis_index("row"), lax.axis_size("row")))
    pl.when(near)(lambda: unpack(src_ref, out, sums_out, src_sems))
    unpack(tgt_ref, tgt_out, tgt_sums_out, sems)


def moves(mesh_shape, axis, keep):
    rows, cols = mesh_shape
    pairs = []
    for r in range(rows):
        for c in range(cols):
            if keep(r):
                to = ((r + 1) % rows, c) if axis == "row" else (r, (c + 1) % cols)
                pairs.append((r * cols + c, to[0] * cols + to[1]))
    return pairs


def on_device(
    source_emb, source_acc, target_emb, target_acc, relations, src_index, dst_index, rel_index, neg_index
):
    src, tgt = source_emb[0, 0].T, target_emb[0, 0].T
    width, entities = src.shape
    types = relations.shape[0]
    edges, negs = src_index.shape[3], neg_index.shape[3]
    block = pltpu.VMEM((width + PAD, entities), f32)
    vmem = pl.BlockSpec(memory_space=pltpu.VMEM)
    hbm = pl.BlockSpec(memory_space=pltpu.HBM)
    params = pltpu.CompilerParams(vmem_limit_bytes=VMEM_LIMIT)

    operands = (src, source_acc, tgt, target_acc, relations.T, src_index, dst_index, rel_index, neg_index)
    operands = [pltpu.with_memory_space_constraint(x, pltpu.HBM) for x in operands]
    mesh_shape = (lax.axis_size("row"), lax.axis_size("col"))
    half = mesh_shape[0] // 2

    def shift(x, axis, keep):
        return lax.ppermute(x, ("row", "col"), moves(mesh_shape, axis, keep))

    def to_far(r):
        return (r + 1) % half == 0

    def from_far(r):
        return r % half == 0

    def first_step(kernel, done):
        return pl.pallas_call(
            kernel,
            name=kernel.__name__,
            out_shape=(
                block,
                block,
                pltpu.VMEM((width, edges), f32),
                pltpu.VMEM((2 + negs // edges, edges), jnp.int32),
            ),
            in_specs=[vmem] * len(done) + [hbm] * len(operands),
            out_specs=(vmem,) * 4,
            scratch_shapes=[pltpu.VMEM(x.shape, x.dtype) for x in operands]
            + [pltpu.VMEM((types, 2 * edges), bf16), pltpu.SemaphoreType.DMA((len(operands) + 1,))],
            compiler_params=params,
            cost_estimate=cost(0.001),
        )(*done, *operands)

    def second_step(kernel, *inputs):
        return pl.pallas_call(
            kernel,
            name=kernel.__name__,
            out_shape=(block, block),
            in_specs=[vmem] * len(inputs),
            out_specs=(vmem, vmem),
            compiler_params=params,
            cost_estimate=cost(0.001),
        )(*inputs)

    tgt, src, operators, index = first_step(early_first_kernel, ())
    far_src = shift(src, "row", to_far)
    tgt, src, operators, index = first_step(late_first_kernel, (tgt, operators, index))
    near_tgt = shift(tgt, "col", lambda r: not from_far(r))
    near_src = shift(src, "row", lambda r: not to_far(r))
    far_tgt = shift(tgt, "col", from_far)
    arrived = pl.pallas_call(
        arrived_kernel,
        name="arrived",
        out_shape=pltpu.VMEM((PAD, entities), f32),
        in_specs=[vmem] * 2,
        out_specs=vmem,
        compiler_params=params,
        cost_estimate=cost(FINAL_COST),
    )(far_src, near_tgt)
    tgt, src = second_step(early_second_kernel, arrived, far_src, near_tgt, near_src, operators, index)
    early_src = src
    tgt, src = second_step(late_second_kernel, tgt, src, far_tgt, far_src, operators, index)
    tgt = shift(tgt, "col", lambda r: True)
    src = shift(src, "row", lambda r: not to_far(r))
    far_src_out = shift(early_src, "row", to_far)
    table = pltpu.HBM((width, entities), f32)
    sums = pltpu.HBM((1, 1, entities), f32)

    out = pl.pallas_call(
        unpack_far_kernel,
        name="unpack_far",
        out_shape=(table, sums),
        in_specs=[vmem],
        out_specs=(hbm,) * 2,
        scratch_shapes=[pltpu.SemaphoreType.DMA((2,))],
        compiler_params=params,
        cost_estimate=cost(FINAL_COST),
    )(far_src_out)
    src, src_sums, tgt, tgt_sums = pl.pallas_call(
        unpack_kernel,
        name="unpack",
        out_shape=(table, sums, table, sums),
        in_specs=[hbm, hbm, vmem, vmem],
        out_specs=(hbm,) * 4,
        input_output_aliases={0: 0, 1: 1},
        scratch_shapes=[pltpu.SemaphoreType.DMA((2,))] * 2,
        compiler_params=params,
        cost_estimate=cost(FINAL_COST),
    )(*out, tgt, src)
    return src.T[None, None], src_sums, tgt.T[None, None], tgt_sums


def solution(mesh):
    grid4 = P("row", "col", None, None)
    grid3 = P("row", "col", None)
    return jax.shard_map(
        on_device,
        mesh=mesh,
        in_specs=(grid4, grid3, grid4, grid3, P(), grid4, grid4, grid4, grid4),
        out_specs=(grid4, grid3, grid4, grid3),
        check_vma=False,
    )
```

```python
import functools

import jax
import jax.numpy as jnp
from jax import lax
from jax.experimental import pallas as pl
from jax.experimental.pallas import tpu as pltpu
from jax.sharding import PartitionSpec as P


learning_rate = 0.1
bf16 = jnp.bfloat16
f32 = jnp.float32
PAD = 8
CHUNK = 512
RUN = 8
LATE_FROM = 5
VMEM_LIMIT = 32 * 1024 * 1024

plain = (((1,), (0,)), ((), ()))
left_t = (((0,), (0,)), ((), ()))
right_t = (((1,), (1,)), ((), ()))


def mm(a, b, dims=plain):
    return lax.dot_general(a, b, dims, preferred_element_type=f32)


def two_parts(x):
    hi = x.astype(bf16)
    lo = (x - hi.astype(f32)).astype(bf16)
    return hi, lo


def one_hot(index_row, size):
    at = lax.broadcasted_iota(jnp.int32, (size, index_row.shape[1]), 0)
    return jnp.where(at == index_row, 1.0, 0.0).astype(f32)


def bucket_step(src, src_sums, tgt, tgt_sums, operators, src_rows, dst_rows, neg_rows):
    width, entities = src.shape
    half = width // 2
    lanes = src_rows.shape[1]
    negs = lanes * len(neg_rows)

    pick_s = one_hot(src_rows, entities).astype(bf16)
    pick_d = one_hot(dst_rows, entities).astype(bf16)
    pick_s2 = jnp.concatenate([pick_s, pick_s], axis=0)
    pick_d2 = jnp.concatenate([pick_d, pick_d], axis=0)
    held = one_hot(neg_rows[0], entities)
    for row in neg_rows[1:]:
        held = held + one_hot(row, entities)
    count_col = jnp.sum(held, axis=1, keepdims=True)
    count_row = mm(jnp.ones((8, lanes), bf16), held.astype(bf16), right_t)[0:1]

    op_re, op_im = operators[:half], operators[half:]
    rows = mm(jnp.concatenate(two_parts(src), axis=1), pick_s2)
    matched = mm(jnp.concatenate(two_parts(tgt), axis=1), pick_d2)
    re, im = rows[:half], rows[half:]
    queries = jnp.concatenate([re * op_re - im * op_im, re * op_im + im * op_re], axis=0)
    positive = jnp.sum(queries * matched, axis=0, keepdims=True)
    pos_grad = -1.0 / (1.0 + jnp.exp(positive))

    queries_b = queries.astype(bf16)
    target_b = tgt.astype(bf16)
    scores = mm(target_b, queries_b, left_t)
    weights = ((1.0 / (1.0 + jnp.exp(-scores))) * (1.0 / negs)).astype(bf16)
    counted = jnp.concatenate(two_parts(weights.astype(f32) * count_col), axis=0)

    pull = mm(jnp.concatenate([target_b, target_b], axis=1), counted)
    grad = pos_grad * matched + pull
    g_re, g_im = grad[:half], grad[half:]
    back = jnp.concatenate([g_re * op_re + g_im * op_im, g_im * op_re - g_re * op_im], axis=0)
    src_grad = mm(
        jnp.concatenate(two_parts(back), axis=1), jnp.concatenate([pick_s, pick_s], axis=1), right_t
    )

    tgt_grad = mm(queries_b, weights, right_t) * count_row + mm(
        jnp.concatenate(two_parts(pos_grad * queries), axis=1),
        jnp.concatenate([pick_d, pick_d], axis=1),
        right_t,
    )

    def adagrad(table, sums, g):
        new_sums = sums + jnp.sum(g * g, axis=0, keepdims=True) * (1.0 / width)
        return table - g * (learning_rate / jnp.sqrt(new_sums)), new_sums

    src, src_sums = adagrad(src, src_sums, src_grad)
    tgt, tgt_sums = adagrad(tgt, tgt_sums, tgt_grad)
    return src, src_sums, tgt, tgt_sums


def store_block(ref, table, sums):
    width = table.shape[0]
    ref[:width, :] = table
    ref[width:, :] = jnp.broadcast_to(sums, (ref.shape[0] - width, sums.shape[1]))


def first_kernel(
    src_hbm, src_sums_hbm, tgt_hbm, tgt_sums_hbm, table_hbm, s_hbm, d_hbm, g_hbm, n_hbm,
    tgt_a_out, src_out, tgt_b_out, op_out, index_out,
    src_ref, src_sums_ref, tgt_ref, tgt_sums_ref, table_ref, s_ref, d_ref, g_ref, n_ref, pick_ref, sems,
):
    width, entities = src_ref.shape
    types = table_ref.shape[1]
    lanes = s_ref.shape[3]
    cut = (width // 2 + 15) // 16 * 16
    parts = [(0, cut), (cut, width - cut)]
    pairs = [(g_hbm, g_ref)]
    pairs += [(table_hbm.at[pl.ds(a, n)], table_ref.at[pl.ds(a, n)]) for a, n in parts]
    pairs += [
        (src_hbm, src_ref), (tgt_hbm, tgt_ref), (s_hbm, s_ref), (d_hbm, d_ref), (n_hbm, n_ref),
        (src_sums_hbm, src_sums_ref), (tgt_sums_hbm, tgt_sums_ref),
    ]
    copies = [pltpu.make_async_copy(a, b, sems.at[i]) for i, (a, b) in enumerate(pairs)]
    for copy in copies:
        copy.start()
    copies[0].wait()
    wanted = jnp.concatenate([g_ref[0, 0, 0:1, :], g_ref[0, 0, 1:2, :]], axis=1)
    for k in range(0, types, CHUNK):
        n = min(CHUNK, types - k)
        pick_ref[k : k + n, :] = one_hot(wanted - k, n).astype(bf16)
    pieces = []
    for copy, (a, n) in zip(copies[1:3], parts):
        copy.wait()
        pieces.append(mm(table_ref[a : a + n, :], pick_ref[...]))
    for copy in copies[3:]:
        copy.wait()
    operators = jnp.concatenate(pieces, axis=0)
    op_out[...] = operators[:, lanes:]
    index_out[0:1, :] = s_ref[0, 0, 1:2, :]
    index_out[1:2, :] = d_ref[0, 0, 1:2, :]
    for k in range(n_ref.shape[3] // lanes):
        index_out[2 + k : 3 + k, :] = n_ref[0, 0, 1:2, k * lanes : (k + 1) * lanes]
    negs = [n_ref[0, 0, 0:1, k * lanes : (k + 1) * lanes] for k in range(n_ref.shape[3] // lanes)]
    src, src_sums, tgt, tgt_sums = bucket_step(
        src_ref[...], src_sums_ref[0], tgt_ref[...], tgt_sums_ref[0], operators[:, :lanes],
        s_ref[0, 0, 0:1, :], d_ref[0, 0, 0:1, :], negs,
    )
    store_block(src_out, src, src_sums)
    store_block(tgt_a_out, tgt, tgt_sums)
    store_block(tgt_b_out, tgt, tgt_sums)


def second_kernel(tgt_a_ref, src_ref, tgt_b_ref, op_ref, index_ref, tgt_a_out, src_out, tgt_b_out):
    width = op_ref.shape[0]
    tgt = jnp.where(from_late(lax.axis_index("col")), tgt_a_ref[...], tgt_b_ref[...])
    negs = [index_ref[k : k + 1, :] for k in range(2, index_ref.shape[0])]
    src, src_sums, tgt, tgt_sums = bucket_step(
        src_ref[:width, :], src_ref[width : width + 1, :], tgt[:width, :], tgt[width : width + 1, :],
        op_ref[...], index_ref[0:1, :], index_ref[1:2, :], negs,
    )
    store_block(src_out, src, src_sums)
    store_block(tgt_a_out, tgt, tgt_sums)
    store_block(tgt_b_out, tgt, tgt_sums)


def late(col):
    return col % RUN >= LATE_FROM


def from_late(col):
    return lax.rem(col + RUN - 1, RUN) >= LATE_FROM


def unpack_kernel(tgt_a_ref, src_ref, tgt_b_ref, src_out, src_sums_out, tgt_out, tgt_sums_out, sems):
    width = src_out.shape[0]

    def send(ref, out, sums_out, first):
        pairs = [(ref.at[pl.ds(0, width)], out), (ref.at[pl.ds(width, 1)], sums_out.at[0])]
        return [pltpu.make_async_copy(a, b, sems.at[first + i]) for i, (a, b) in enumerate(pairs)]

    def move(tgt_ref):
        copies = send(src_ref, src_out, src_sums_out, 0) + send(tgt_ref, tgt_out, tgt_sums_out, 2)
        for copy in copies:
            copy.start()
        for copy in copies:
            copy.wait()

    a = from_late(lax.axis_index("col"))
    pl.when(a)(lambda: move(tgt_a_ref))
    pl.when(jnp.logical_not(a))(lambda: move(tgt_b_ref))


def shift(x, axis, keep=None):
    length = lax.axis_size(axis)
    return lax.ppermute(x, axis, [(i, (i + 1) % length) for i in range(length) if keep is None or keep(i)])


def early(col):
    return not late(col)


def on_device(
    source_emb, source_acc, target_emb, target_acc, relations, src_index, dst_index, rel_index, neg_index
):
    src, tgt = source_emb[0, 0].T, target_emb[0, 0].T
    width, entities = src.shape
    types = relations.shape[0]
    edges, negs = src_index.shape[3], neg_index.shape[3]
    block = pltpu.VMEM((width + PAD, entities), f32)
    vmem = pl.BlockSpec(memory_space=pltpu.VMEM)
    hbm = pl.BlockSpec(memory_space=pltpu.HBM)
    params = pltpu.CompilerParams(vmem_limit_bytes=VMEM_LIMIT)

    operands = (src, source_acc, tgt, target_acc, relations.T, src_index, dst_index, rel_index, neg_index)
    tgt_a, src, tgt_b, operators, index = pl.pallas_call(
        first_kernel,
        name="first_step",
        out_shape=(
            block,
            block,
            block,
            pltpu.VMEM((width, edges), f32),
            pltpu.VMEM((2 + negs // edges, edges), jnp.int32),
        ),
        in_specs=[hbm] * len(operands),
        out_specs=(vmem,) * 5,
        scratch_shapes=[pltpu.VMEM(x.shape, x.dtype) for x in operands]
        + [pltpu.VMEM((types, 2 * edges), bf16), pltpu.SemaphoreType.DMA((len(operands) + 1,))],
        compiler_params=params,
    )(*[pltpu.with_memory_space_constraint(x, pltpu.HBM) for x in operands])
    tgt_a = shift(tgt_a, "col", late)
    src = shift(src, "row")
    tgt_b = shift(tgt_b, "col", early)
    tgt_a, src, tgt_b = pl.pallas_call(
        second_kernel,
        name="second_step",
        out_shape=(block, block, block),
        in_specs=[vmem] * 5,
        out_specs=(vmem,) * 3,
        compiler_params=params,
    )(tgt_a, src, tgt_b, operators, index)
    tgt_a = shift(tgt_a, "col", late)
    src = shift(src, "row")
    tgt_b = shift(tgt_b, "col", early)
    table = pltpu.HBM((width, entities), f32)
    sums = pltpu.HBM((1, 1, entities), f32)
    src, src_sums, tgt, tgt_sums = pl.pallas_call(
        unpack_kernel,
        name="unpack",
        out_shape=(table, sums, table, sums),
        in_specs=[vmem] * 3,
        out_specs=(hbm,) * 4,
        scratch_shapes=[pltpu.SemaphoreType.DMA((4,))],
        compiler_params=params,
    )(tgt_a, src, tgt_b)
    return src.T[None, None], src_sums, tgt.T[None, None], tgt_sums


def solution(mesh):
    grid4 = P("row", "col", None, None)
    grid3 = P("row", "col", None)
    return jax.shard_map(
        on_device,
        mesh=mesh,
        in_specs=(grid4, grid3, grid4, grid3, P(), grid4, grid4, grid4, grid4),
        out_specs=(grid4, grid3, grid4, grid3),
        check_vma=False,
    )
```

```python
import functools

import jax
import jax.numpy as jnp
from jax import lax
from jax.experimental import pallas as pl
from jax.experimental.pallas import tpu as pltpu
from jax.sharding import PartitionSpec as P


learning_rate = 0.1
bf16 = jnp.bfloat16
f32 = jnp.float32
PAD = 8
CHUNK = 512
RUN = 8
LATE_FIRST = 6
LATE_SECOND = 7
VMEM_LIMIT = 32 * 1024 * 1024

plain = (((1,), (0,)), ((), ()))
left_t = (((0,), (0,)), ((), ()))
right_t = (((1,), (1,)), ((), ()))


def mm(a, b, dims=plain):
    return lax.dot_general(a, b, dims, preferred_element_type=f32)


def two_parts(x):
    hi = x.astype(bf16)
    lo = (x - hi.astype(f32)).astype(bf16)
    return hi, lo


def one_hot(index_row, size):
    at = lax.broadcasted_iota(jnp.int32, (size, index_row.shape[1]), 0)
    return jnp.where(at == index_row, 1.0, 0.0).astype(f32)


def count_rows(neg_rows, entities):
    held = one_hot(neg_rows[0], entities)
    for row in neg_rows[1:]:
        held = held + one_hot(row, entities)
    return mm(jnp.ones((8, held.shape[1]), bf16), held.astype(bf16), right_t)[0:1]


def bucket_step(src, src_sums, tgt, tgt_sums, operators, src_rows, dst_rows, counts, negs):
    width, entities = src.shape
    half = width // 2

    pick_s = one_hot(src_rows, entities).astype(bf16)
    pick_d = one_hot(dst_rows, entities).astype(bf16)
    op_re, op_im = operators[:half], operators[half:]
    rows = mm(jnp.concatenate(two_parts(src), axis=1), jnp.concatenate([pick_s, pick_s], axis=0))
    matched = mm(jnp.concatenate(two_parts(tgt), axis=1), jnp.concatenate([pick_d, pick_d], axis=0))
    re, im = rows[:half], rows[half:]
    queries = jnp.concatenate([re * op_re - im * op_im, re * op_im + im * op_re], axis=0)
    positive = jnp.sum(queries * matched, axis=0, keepdims=True)
    pos_grad = -1.0 / (1.0 + jnp.exp(positive))

    queries_b = queries.astype(bf16)
    target_b = tgt.astype(bf16)
    scores = mm(target_b, queries_b, left_t)
    weights = ((1.0 / (1.0 + jnp.exp(-scores))) * (1.0 / negs)).astype(bf16)

    counted = jnp.concatenate(two_parts(target_b.astype(f32) * counts), axis=1)
    pull = mm(counted, jnp.concatenate([weights, weights], axis=0))
    grad = pos_grad * matched + pull
    g_re, g_im = grad[:half], grad[half:]
    back = jnp.concatenate([g_re * op_re + g_im * op_im, g_im * op_re - g_re * op_im], axis=0)
    src_grad = mm(
        jnp.concatenate(two_parts(back), axis=1), jnp.concatenate([pick_s, pick_s], axis=1), right_t
    )

    tgt_grad = mm(queries_b, weights, right_t) * counts + mm(
        jnp.concatenate(two_parts(pos_grad * queries), axis=1),
        jnp.concatenate([pick_d, pick_d], axis=1),
        right_t,
    )

    def adagrad(table, sums, g):
        new_sums = sums + jnp.sum(g * g, axis=0, keepdims=True) * (1.0 / width)
        return table - g * (learning_rate / jnp.sqrt(new_sums)), new_sums

    src, src_sums = adagrad(src, src_sums, src_grad)
    tgt, tgt_sums = adagrad(tgt, tgt_sums, tgt_grad)
    return src, src_sums, tgt, tgt_sums


def store_block(ref, table, sums):
    width = table.shape[0]
    ref[:width, :] = table
    ref[width:, :] = jnp.broadcast_to(sums, (ref.shape[0] - width, sums.shape[1]))


def first_kernel(
    src_hbm, src_sums_hbm, tgt_hbm, tgt_sums_hbm, table_hbm, s_hbm, d_hbm, g_hbm, n_hbm,
    tgt_a_out, src_out, move_out, tgt_b_out, own_out,
    src_ref, src_sums_ref, tgt_ref, tgt_sums_ref, table_ref, s_ref, d_ref, g_ref, n_ref, pick_ref, sems,
):
    width, entities = src_ref.shape
    types = table_ref.shape[1]
    lanes = s_ref.shape[3]
    cut = (width // 2 + 15) // 16 * 16
    parts = [(0, cut), (cut, width - cut)]
    pairs = [(g_hbm, g_ref)]
    pairs += [(table_hbm.at[pl.ds(a, n)], table_ref.at[pl.ds(a, n)]) for a, n in parts]
    pairs += [
        (src_hbm, src_ref), (tgt_hbm, tgt_ref), (s_hbm, s_ref), (d_hbm, d_ref), (n_hbm, n_ref),
        (src_sums_hbm, src_sums_ref), (tgt_sums_hbm, tgt_sums_ref),
    ]
    copies = [pltpu.make_async_copy(a, b, sems.at[i]) for i, (a, b) in enumerate(pairs)]
    for copy in copies:
        copy.start()
    copies[0].wait()
    wanted = jnp.concatenate([g_ref[0, 0, 0:1, :], g_ref[0, 0, 1:2, :]], axis=1)
    for k in range(0, types, CHUNK):
        n = min(CHUNK, types - k)
        pick_ref[k : k + n, :] = one_hot(wanted - k, n).astype(bf16)
    pieces = []
    for copy, (a, n) in zip(copies[1:3], parts):
        copy.wait()
        pieces.append(mm(table_ref[a : a + n, :], pick_ref[...]))
    for copy in copies[3:]:
        copy.wait()
    operators = jnp.concatenate(pieces, axis=0)
    negs = n_ref.shape[3]
    counts = [
        count_rows([n_ref[0, 0, t : t + 1, k : k + lanes] for k in range(0, negs, lanes)], src_ref.shape[1])
        for t in range(2)
    ]
    index = [s_ref[0, 0, 1:2, :].astype(f32), d_ref[0, 0, 1:2, :].astype(f32), counts[1]]
    index = jnp.concatenate(index + [jnp.zeros((PAD - len(index), lanes), f32)], axis=0)
    for out in (move_out, own_out):
        out[:width, :] = operators[:, lanes:]
        out[width:, :] = index
    src, src_sums, tgt, tgt_sums = bucket_step(
        src_ref[...], src_sums_ref[0], tgt_ref[...], tgt_sums_ref[0], operators[:, :lanes],
        s_ref[0, 0, 0:1, :], d_ref[0, 0, 0:1, :], counts[0], negs,
    )
    store_block(src_out, src, src_sums)
    store_block(tgt_a_out, tgt, tgt_sums)
    store_block(tgt_b_out, tgt, tgt_sums)


def second_kernel(negs, tgt_a_ref, src_ref, moved_ref, tgt_b_ref, own_ref, tgt_a_out, src_out, tgt_b_out):
    row, col = lax.axis_index("row"), lax.axis_index("col")
    width = src_ref.shape[0] - PAD
    tgt = jnp.where(from_late(col, LATE_FIRST), tgt_a_ref[...], tgt_b_ref[...])
    pack = jnp.where(takes_moved(row, col, lax.axis_size("row")), moved_ref[...], own_ref[...])
    src, src_sums, tgt, tgt_sums = bucket_step(
        src_ref[:width, :], src_ref[width : width + 1, :], tgt[:width], tgt[width : width + 1], pack[:width],
        pack[width : width + 1].astype(jnp.int32), pack[width + 1 : width + 2].astype(jnp.int32),
        pack[width + 2 : width + 3], negs,
    )
    store_block(src_out, src, src_sums)
    store_block(tgt_a_out, tgt, tgt_sums)
    store_block(tgt_b_out, tgt, tgt_sums)


def from_late(col, late):
    return lax.rem(col + RUN - 1, RUN) >= late


def takes_moved(row, col, rows):
    z = lax.rem(col, RUN)
    return jnp.logical_or(z == 0, jnp.logical_and(z == RUN - 1, lax.rem(row, rows // 2) == 0))


def place(row, col, rows, cols):
    group, z = divmod(col, RUN)
    if z == 0:
        group -= 1
    elif z == RUN - 1 and row % (rows // 2) == 0:
        group += 1
    return row, group % (cols // RUN) * RUN + z


def unpack_kernel(tgt_a_ref, src_ref, tgt_b_ref, src_out, src_sums_out, tgt_out, tgt_sums_out, sems):
    width = src_out.shape[0]

    def send(ref, out, sums_out, first):
        pairs = [(ref.at[pl.ds(0, width)], out), (ref.at[pl.ds(width, 1)], sums_out.at[0])]
        return [pltpu.make_async_copy(a, b, sems.at[first + i]) for i, (a, b) in enumerate(pairs)]

    def move(tgt_ref):
        copies = send(src_ref, src_out, src_sums_out, 0) + send(tgt_ref, tgt_out, tgt_sums_out, 2)
        for copy in copies:
            copy.start()
        for copy in copies:
            copy.wait()

    a = from_late(lax.axis_index("col"), LATE_SECOND)
    pl.when(a)(lambda: move(tgt_a_ref))
    pl.when(jnp.logical_not(a))(lambda: move(tgt_b_ref))


def routes(rows, cols):
    def pairs(source, target, keep=lambda r, c: True):
        found = []
        for r in range(rows):
            for c in range(cols):
                (r0, c0), (r1, c1) = source(r, c), target(r, c)
                if keep(r, c):
                    found.append((r0 * cols + c0, r1 * cols + c1))
        return found

    def home(r, c):
        return r, c

    def there(r, c):
        return place(r, c, rows, cols)

    def back_row(r, c):
        return (r - 1) % rows, c

    def back_col(r, c):
        return r, (c - 1) % cols

    def next_row(r, c):
        return (r + 1) % rows, c

    def next_col(r, c):
        return r, (c + 1) % cols

    def late_first(r, c):
        return (c - 1) % RUN >= LATE_FIRST

    def late_second(r, c):
        return c % RUN >= LATE_SECOND

    def negate(f):
        return lambda r, c: not f(r, c)

    return {
        "first_tgt_a": pairs(back_col, there, late_first),
        "first_src": pairs(back_row, there),
        "moved": pairs(home, there, lambda r, c: there(r, c) != (r, c)),
        "first_tgt_b": pairs(back_col, there, negate(late_first)),
        "second_tgt_a": pairs(there, next_col, late_second),
        "second_src": pairs(there, next_row),
        "second_tgt_b": pairs(there, next_col, negate(late_second)),
    }


def on_device(
    source_emb, source_acc, target_emb, target_acc, relations, src_index, dst_index, rel_index, neg_index
):
    src, tgt = source_emb[0, 0].T, target_emb[0, 0].T
    width, entities = src.shape
    types = relations.shape[0]
    edges, negs = src_index.shape[3], neg_index.shape[3]
    block = pltpu.VMEM((width + PAD, entities), f32)
    route = routes(lax.axis_size("row"), lax.axis_size("col"))

    def send(x, name):
        return lax.ppermute(x, ("row", "col"), route[name])

    vmem = pl.BlockSpec(memory_space=pltpu.VMEM)
    hbm = pl.BlockSpec(memory_space=pltpu.HBM)
    params = pltpu.CompilerParams(vmem_limit_bytes=VMEM_LIMIT)

    operands = (src, source_acc, tgt, target_acc, relations.T, src_index, dst_index, rel_index, neg_index)
    tgt_a, src, moved, tgt_b, own = pl.pallas_call(
        first_kernel,
        name="first_step",
        out_shape=(
            block,
            block,
            block,
            block,
            block,
        ),
        in_specs=[hbm] * len(operands),
        out_specs=(vmem,) * 5,
        scratch_shapes=[pltpu.VMEM(x.shape, x.dtype) for x in operands]
        + [pltpu.VMEM((types, 2 * edges), bf16), pltpu.SemaphoreType.DMA((len(operands) + 1,))],
        compiler_params=params,
    )(*[pltpu.with_memory_space_constraint(x, pltpu.HBM) for x in operands])
    tgt_a = send(tgt_a, "first_tgt_a")
    src = send(src, "first_src")
    moved = send(moved, "moved")
    tgt_b = send(tgt_b, "first_tgt_b")
    tgt_a, src, tgt_b = pl.pallas_call(
        functools.partial(second_kernel, negs),
        name="second_step",
        out_shape=(block, block, block),
        in_specs=[vmem] * 5,
        out_specs=(vmem,) * 3,
        compiler_params=params,
    )(tgt_a, src, moved, tgt_b, own)
    tgt_a = send(tgt_a, "second_tgt_a")
    src = send(src, "second_src")
    tgt_b = send(tgt_b, "second_tgt_b")
    table = pltpu.HBM((width, entities), f32)
    sums = pltpu.HBM((1, 1, entities), f32)
    src, src_sums, tgt, tgt_sums = pl.pallas_call(
        unpack_kernel,
        name="unpack",
        out_shape=(table, sums, table, sums),
        in_specs=[vmem] * 3,
        out_specs=(hbm,) * 4,
        scratch_shapes=[pltpu.SemaphoreType.DMA((4,))],
        compiler_params=params,
    )(tgt_a, src, tgt_b)
    return src.T[None, None], src_sums, tgt.T[None, None], tgt_sums


def solution(mesh):
    grid4 = P("row", "col", None, None)
    grid3 = P("row", "col", None)
    return jax.shard_map(
        on_device,
        mesh=mesh,
        in_specs=(grid4, grid3, grid4, grid3, P(), grid4, grid4, grid4, grid4),
        out_specs=(grid4, grid3, grid4, grid3),
        check_vma=False,
    )
```

```python
import functools

import jax
import jax.numpy as jnp
from jax import lax
from jax.experimental import pallas as pl
from jax.experimental.pallas import tpu as pltpu
from jax.sharding import PartitionSpec as P


learning_rate = 0.1
bf16 = jnp.bfloat16
f32 = jnp.float32
PAD = 8
CHUNK = 512
RUN = 8
LATE_FIRST = 5
LATE_SECOND = 5
VMEM_LIMIT = 32 * 1024 * 1024

plain = (((1,), (0,)), ((), ()))
left_t = (((0,), (0,)), ((), ()))
right_t = (((1,), (1,)), ((), ()))


def mm(a, b, dims=plain):
    return lax.dot_general(a, b, dims, preferred_element_type=f32)


def two_parts(x):
    hi = x.astype(bf16)
    lo = (x - hi.astype(f32)).astype(bf16)
    return hi, lo


def one_hot(index_row, size):
    at = lax.broadcasted_iota(jnp.int32, (size, index_row.shape[1]), 0)
    return jnp.where(at == index_row, 1.0, 0.0).astype(f32)


def count_rows(neg_rows, entities):
    held = one_hot(neg_rows[0], entities)
    for row in neg_rows[1:]:
        held = held + one_hot(row, entities)
    return mm(jnp.ones((8, held.shape[1]), bf16), held.astype(bf16), right_t)[0:1]


def bucket_step(src, src_sums, tgt, tgt_sums, operators, src_rows, dst_rows, counts, negs):
    width, entities = src.shape
    half = width // 2

    pick_s = one_hot(src_rows, entities).astype(bf16)
    pick_d = one_hot(dst_rows, entities).astype(bf16)
    op_re, op_im = operators[:half], operators[half:]
    rows = mm(jnp.concatenate(two_parts(src), axis=1), jnp.concatenate([pick_s, pick_s], axis=0))
    matched = mm(jnp.concatenate(two_parts(tgt), axis=1), jnp.concatenate([pick_d, pick_d], axis=0))
    re, im = rows[:half], rows[half:]
    queries = jnp.concatenate([re * op_re - im * op_im, re * op_im + im * op_re], axis=0)
    positive = jnp.sum(queries * matched, axis=0, keepdims=True)
    pos_grad = -1.0 / (1.0 + jnp.exp(positive))

    queries_b = queries.astype(bf16)
    target_b = tgt.astype(bf16)
    scores = mm(target_b, queries_b, left_t)
    weights = ((1.0 / (1.0 + jnp.exp(-scores))) * (1.0 / negs)).astype(bf16)

    counted = jnp.concatenate(two_parts(target_b.astype(f32) * counts), axis=1)
    pull = mm(counted, jnp.concatenate([weights, weights], axis=0))
    grad = pos_grad * matched + pull
    g_re, g_im = grad[:half], grad[half:]
    back = jnp.concatenate([g_re * op_re + g_im * op_im, g_im * op_re - g_re * op_im], axis=0)
    src_grad = mm(
        jnp.concatenate(two_parts(back), axis=1), jnp.concatenate([pick_s, pick_s], axis=1), right_t
    )

    tgt_grad = mm(queries_b, weights, right_t) * counts + mm(
        jnp.concatenate(two_parts(pos_grad * queries), axis=1),
        jnp.concatenate([pick_d, pick_d], axis=1),
        right_t,
    )

    def adagrad(table, sums, g):
        new_sums = sums + jnp.sum(g * g, axis=0, keepdims=True) * (1.0 / width)
        return table - g * (learning_rate / jnp.sqrt(new_sums)), new_sums

    src, src_sums = adagrad(src, src_sums, src_grad)
    tgt, tgt_sums = adagrad(tgt, tgt_sums, tgt_grad)
    return src, src_sums, tgt, tgt_sums


def store_block(ref, table, sums):
    width = table.shape[0]
    ref[:width, :] = table
    ref[width:, :] = jnp.broadcast_to(sums, (ref.shape[0] - width, sums.shape[1]))


def first_kernel(
    src_hbm, src_sums_hbm, tgt_hbm, tgt_sums_hbm, table_hbm, s_hbm, d_hbm, g_hbm, n_hbm,
    tgt_a_out, src_out, move_out, tgt_b_out, own_out,
    src_ref, src_sums_ref, tgt_ref, tgt_sums_ref, table_ref, s_ref, d_ref, g_ref, n_ref, pick_ref, sems,
):
    width, entities = src_ref.shape
    types = table_ref.shape[1]
    lanes = s_ref.shape[3]
    cut = (width // 2 + 15) // 16 * 16
    parts = [(0, cut), (cut, width - cut)]
    pairs = [(g_hbm, g_ref)]
    pairs += [(table_hbm.at[pl.ds(a, n)], table_ref.at[pl.ds(a, n)]) for a, n in parts]
    pairs += [
        (src_hbm, src_ref), (tgt_hbm, tgt_ref), (s_hbm, s_ref), (d_hbm, d_ref), (n_hbm, n_ref),
        (src_sums_hbm, src_sums_ref), (tgt_sums_hbm, tgt_sums_ref),
    ]
    copies = [pltpu.make_async_copy(a, b, sems.at[i]) for i, (a, b) in enumerate(pairs)]
    for copy in copies:
        copy.start()
    copies[0].wait()
    wanted = jnp.concatenate([g_ref[0, 0, 0:1, :], g_ref[0, 0, 1:2, :]], axis=1)
    for k in range(0, types, CHUNK):
        n = min(CHUNK, types - k)
        pick_ref[k : k + n, :] = one_hot(wanted - k, n).astype(bf16)
    pieces = []
    for copy, (a, n) in zip(copies[1:3], parts):
        copy.wait()
        pieces.append(mm(table_ref[a : a + n, :], pick_ref[...]))
    for copy in copies[3:]:
        copy.wait()
    operators = jnp.concatenate(pieces, axis=0)
    negs = n_ref.shape[3]
    counts = [
        count_rows([n_ref[0, 0, t : t + 1, k : k + lanes] for k in range(0, negs, lanes)], src_ref.shape[1])
        for t in range(2)
    ]
    index = [s_ref[0, 0, 1:2, :].astype(f32), d_ref[0, 0, 1:2, :].astype(f32), counts[1]]
    index = jnp.concatenate(index + [jnp.zeros((PAD - len(index), lanes), f32)], axis=0)
    for out in (move_out, own_out):
        out[:width, :] = operators[:, lanes:]
        out[width:, :] = index
    src, src_sums, tgt, tgt_sums = bucket_step(
        src_ref[...], src_sums_ref[0], tgt_ref[...], tgt_sums_ref[0], operators[:, :lanes],
        s_ref[0, 0, 0:1, :], d_ref[0, 0, 0:1, :], counts[0], negs,
    )
    store_block(src_out, src, src_sums)
    store_block(tgt_a_out, tgt, tgt_sums)
    store_block(tgt_b_out, tgt, tgt_sums)


def second_kernel(negs, tgt_a_ref, src_ref, moved_ref, tgt_b_ref, own_ref, tgt_a_out, src_out, tgt_b_out):
    row, col = lax.axis_index("row"), lax.axis_index("col")
    width = src_ref.shape[0] - PAD
    tgt = jnp.where(from_late(col, LATE_FIRST), tgt_a_ref[...], tgt_b_ref[...])
    pack = jnp.where(takes_moved(row, col, lax.axis_size("row")), moved_ref[...], own_ref[...])
    src, src_sums, tgt, tgt_sums = bucket_step(
        src_ref[:width, :], src_ref[width : width + 1, :], tgt[:width], tgt[width : width + 1], pack[:width],
        pack[width : width + 1].astype(jnp.int32), pack[width + 1 : width + 2].astype(jnp.int32),
        pack[width + 2 : width + 3], negs,
    )
    store_block(src_out, src, src_sums)
    store_block(tgt_a_out, tgt, tgt_sums)
    store_block(tgt_b_out, tgt, tgt_sums)


def from_late(col, late):
    return lax.rem(col + RUN - 1, RUN) >= late


def crosses(row, rows):
    return (row + 1) % (rows // 2) == 0


def takes_moved(row, col, rows):
    return jnp.logical_and(lax.rem(col, RUN) == 0, lax.rem(row + 1, rows // 2) == 0)


def place(row, col, rows, cols):
    group, z = divmod(col, RUN)
    if z == 0 and crosses(row, rows):
        group -= 1
    return row, group % (cols // RUN) * RUN + z


def unpack_kernel(tgt_a_ref, src_ref, tgt_b_ref, src_out, src_sums_out, tgt_out, tgt_sums_out, sems):
    width = src_out.shape[0]

    def send(ref, out, sums_out, first):
        pairs = [(ref.at[pl.ds(0, width)], out), (ref.at[pl.ds(width, 1)], sums_out.at[0])]
        return [pltpu.make_async_copy(a, b, sems.at[first + i]) for i, (a, b) in enumerate(pairs)]

    def move(tgt_ref):
        copies = send(src_ref, src_out, src_sums_out, 0) + send(tgt_ref, tgt_out, tgt_sums_out, 2)
        for copy in copies:
            copy.start()
        for copy in copies:
            copy.wait()

    row, col = lax.axis_index("row"), lax.axis_index("col")
    from_moved = jnp.logical_and(lax.rem(col, RUN) == 1, lax.rem(row + 1, lax.axis_size("row") // 2) == 0)
    a = jnp.logical_or(from_late(col, LATE_SECOND), from_moved)
    pl.when(a)(lambda: move(tgt_a_ref))
    pl.when(jnp.logical_not(a))(lambda: move(tgt_b_ref))


def routes(rows, cols):
    def pairs(source, target, keep=lambda r, c: True):
        found = []
        for r in range(rows):
            for c in range(cols):
                (r0, c0), (r1, c1) = source(r, c), target(r, c)
                if keep(r, c):
                    found.append((r0 * cols + c0, r1 * cols + c1))
        return found

    def home(r, c):
        return r, c

    def there(r, c):
        return place(r, c, rows, cols)

    def back_row(r, c):
        return (r - 1) % rows, c

    def back_col(r, c):
        return r, (c - 1) % cols

    def next_row(r, c):
        return (r + 1) % rows, c

    def next_col(r, c):
        return r, (c + 1) % cols

    def late_first(r, c):
        return (c - 1) % RUN >= LATE_FIRST

    def late_second(r, c):
        return c % RUN >= LATE_SECOND or (c % RUN == 0 and crosses(r, rows))

    def negate(f):
        return lambda r, c: not f(r, c)

    return {
        "first_tgt_a": pairs(back_col, there, late_first),
        "first_src": pairs(back_row, there),
        "moved": pairs(home, there, lambda r, c: there(r, c) != (r, c)),
        "first_tgt_b": pairs(back_col, there, negate(late_first)),
        "second_tgt_a": pairs(there, next_col, late_second),
        "second_src": pairs(there, next_row),
        "second_tgt_b": pairs(there, next_col, negate(late_second)),
    }


def on_device(
    source_emb, source_acc, target_emb, target_acc, relations, src_index, dst_index, rel_index, neg_index
):
    src, tgt = source_emb[0, 0].T, target_emb[0, 0].T
    width, entities = src.shape
    types = relations.shape[0]
    edges, negs = src_index.shape[3], neg_index.shape[3]
    block = pltpu.VMEM((width + PAD, entities), f32)
    route = routes(lax.axis_size("row"), lax.axis_size("col"))

    def send(x, name):
        return lax.ppermute(x, ("row", "col"), route[name])

    vmem = pl.BlockSpec(memory_space=pltpu.VMEM)
    hbm = pl.BlockSpec(memory_space=pltpu.HBM)
    params = pltpu.CompilerParams(vmem_limit_bytes=VMEM_LIMIT)

    operands = (src, source_acc, tgt, target_acc, relations.T, src_index, dst_index, rel_index, neg_index)
    tgt_a, src, moved, tgt_b, own = pl.pallas_call(
        first_kernel,
        name="first_step",
        out_shape=(
            block,
            block,
            block,
            block,
            block,
        ),
        in_specs=[hbm] * len(operands),
        out_specs=(vmem,) * 5,
        scratch_shapes=[pltpu.VMEM(x.shape, x.dtype) for x in operands]
        + [pltpu.VMEM((types, 2 * edges), bf16), pltpu.SemaphoreType.DMA((len(operands) + 1,))],
        compiler_params=params,
    )(*[pltpu.with_memory_space_constraint(x, pltpu.HBM) for x in operands])
    tgt_a = send(tgt_a, "first_tgt_a")
    src = send(src, "first_src")
    moved = send(moved, "moved")
    tgt_b = send(tgt_b, "first_tgt_b")
    tgt_a, src, tgt_b = pl.pallas_call(
        functools.partial(second_kernel, negs),
        name="second_step",
        out_shape=(block, block, block),
        in_specs=[vmem] * 5,
        out_specs=(vmem,) * 3,
        compiler_params=params,
    )(tgt_a, src, moved, tgt_b, own)
    tgt_a = send(tgt_a, "second_tgt_a")
    src = send(src, "second_src")
    tgt_b = send(tgt_b, "second_tgt_b")
    table = pltpu.HBM((width, entities), f32)
    sums = pltpu.HBM((1, 1, entities), f32)
    src, src_sums, tgt, tgt_sums = pl.pallas_call(
        unpack_kernel,
        name="unpack",
        out_shape=(table, sums, table, sums),
        in_specs=[vmem] * 3,
        out_specs=(hbm,) * 4,
        scratch_shapes=[pltpu.SemaphoreType.DMA((4,))],
        compiler_params=params,
    )(tgt_a, src, tgt_b)
    return src.T[None, None], src_sums, tgt.T[None, None], tgt_sums


def solution(mesh):
    grid4 = P("row", "col", None, None)
    grid3 = P("row", "col", None)
    return jax.shard_map(
        on_device,
        mesh=mesh,
        in_specs=(grid4, grid3, grid4, grid3, P(), grid4, grid4, grid4, grid4),
        out_specs=(grid4, grid3, grid4, grid3),
        check_vma=False,
    )
```

```python
import functools

import jax
import jax.numpy as jnp
from jax import lax
from jax.experimental import pallas as pl
from jax.experimental.pallas import tpu as pltpu
from jax.sharding import PartitionSpec as P


learning_rate = 0.1
bf16 = jnp.bfloat16
f32 = jnp.float32
PAD = 8
CHUNK = 512
RUN = 8
LATE_FIRST = 5
LATE_SECOND = 5
VMEM_LIMIT = 32 * 1024 * 1024

plain = (((1,), (0,)), ((), ()))
left_t = (((0,), (0,)), ((), ()))
right_t = (((1,), (1,)), ((), ()))


def mm(a, b, dims=plain):
    return lax.dot_general(a, b, dims, preferred_element_type=f32)


def two_parts(x):
    hi = x.astype(bf16)
    lo = (x - hi.astype(f32)).astype(bf16)
    return hi, lo


def one_hot(index_row, size):
    at = lax.broadcasted_iota(jnp.int32, (size, index_row.shape[1]), 0)
    return jnp.where(at == index_row, 1.0, 0.0).astype(f32)


def count_rows(neg_rows, entities):
    held = one_hot(neg_rows[0], entities)
    for row in neg_rows[1:]:
        held = held + one_hot(row, entities)
    return mm(jnp.ones((8, held.shape[1]), bf16), held.astype(bf16), right_t)[0:1]


def bucket_step(src, src_sums, tgt, tgt_sums, operators, src_rows, dst_rows, counts, negs):
    width, entities = src.shape
    half = width // 2

    pick_s = one_hot(src_rows, entities).astype(bf16)
    pick_d = one_hot(dst_rows, entities).astype(bf16)
    op_re, op_im = operators[:half], operators[half:]
    rows = mm(jnp.concatenate(two_parts(src), axis=1), jnp.concatenate([pick_s, pick_s], axis=0))
    matched = mm(jnp.concatenate(two_parts(tgt), axis=1), jnp.concatenate([pick_d, pick_d], axis=0))
    re, im = rows[:half], rows[half:]
    queries = jnp.concatenate([re * op_re - im * op_im, re * op_im + im * op_re], axis=0)
    positive = jnp.sum(queries * matched, axis=0, keepdims=True)
    pos_grad = -1.0 / (1.0 + jnp.exp(positive))

    queries_b = queries.astype(bf16)
    target_b = tgt.astype(bf16)
    scores = mm(target_b, queries_b, left_t)
    weights = ((1.0 / (1.0 + jnp.exp(-scores))) * (1.0 / negs)).astype(bf16)

    counted = jnp.concatenate(two_parts(target_b.astype(f32) * counts), axis=1)
    pull = mm(counted, jnp.concatenate([weights, weights], axis=0))
    grad = pos_grad * matched + pull
    g_re, g_im = grad[:half], grad[half:]
    back = jnp.concatenate([g_re * op_re + g_im * op_im, g_im * op_re - g_re * op_im], axis=0)
    src_grad = mm(
        jnp.concatenate(two_parts(back), axis=1), jnp.concatenate([pick_s, pick_s], axis=1), right_t
    )

    tgt_grad = mm(queries_b, weights, right_t) * counts + mm(
        jnp.concatenate(two_parts(pos_grad * queries), axis=1),
        jnp.concatenate([pick_d, pick_d], axis=1),
        right_t,
    )

    def adagrad(table, sums, g):
        new_sums = sums + jnp.sum(g * g, axis=0, keepdims=True) * (1.0 / width)
        return table - g * (learning_rate / jnp.sqrt(new_sums)), new_sums

    src, src_sums = adagrad(src, src_sums, src_grad)
    tgt, tgt_sums = adagrad(tgt, tgt_sums, tgt_grad)
    return src, src_sums, tgt, tgt_sums


def store_block(ref, table, sums):
    width = table.shape[0]
    ref[:width, :] = table
    ref[width:, :] = jnp.broadcast_to(sums, (ref.shape[0] - width, sums.shape[1]))


def first_kernel(
    src_hbm, src_sums_hbm, tgt_hbm, tgt_sums_hbm, table_hbm, s_hbm, d_hbm, g_hbm, n_hbm,
    tgt_a_out, src_out, move_out, tgt_b_out, own_out,
    src_ref, src_sums_ref, tgt_ref, tgt_sums_ref, table_ref, s_ref, d_ref, g_ref, n_ref, pick_ref, sems,
):
    width, entities = src_ref.shape
    types = table_ref.shape[1]
    lanes = s_ref.shape[3]
    cut = (width // 2 + 15) // 16 * 16
    parts = [(0, cut), (cut, width - cut)]
    pairs = [(g_hbm, g_ref)]
    pairs += [(table_hbm.at[pl.ds(a, n)], table_ref.at[pl.ds(a, n)]) for a, n in parts]
    pairs += [
        (src_hbm, src_ref), (tgt_hbm, tgt_ref), (s_hbm, s_ref), (d_hbm, d_ref), (n_hbm, n_ref),
        (src_sums_hbm, src_sums_ref), (tgt_sums_hbm, tgt_sums_ref),
    ]
    copies = [pltpu.make_async_copy(a, b, sems.at[i]) for i, (a, b) in enumerate(pairs)]
    for copy in copies:
        copy.start()
    copies[0].wait()
    wanted = jnp.concatenate([g_ref[0, 0, 0:1, :], g_ref[0, 0, 1:2, :]], axis=1)
    for k in range(0, types, CHUNK):
        n = min(CHUNK, types - k)
        pick_ref[k : k + n, :] = one_hot(wanted - k, n).astype(bf16)
    pieces = []
    for copy, (a, n) in zip(copies[1:3], parts):
        copy.wait()
        pieces.append(mm(table_ref[a : a + n, :], pick_ref[...]))
    for copy in copies[3:]:
        copy.wait()
    operators = jnp.concatenate(pieces, axis=0)
    negs = n_ref.shape[3]
    counts = [
        count_rows([n_ref[0, 0, t : t + 1, k : k + lanes] for k in range(0, negs, lanes)], src_ref.shape[1])
        for t in range(2)
    ]
    index = [s_ref[0, 0, 1:2, :].astype(f32), d_ref[0, 0, 1:2, :].astype(f32), counts[1]]
    index = jnp.concatenate(index + [jnp.zeros((PAD - len(index), lanes), f32)], axis=0)
    for out in (move_out, own_out):
        out[:width, :] = operators[:, lanes:]
        out[width:, :] = index
    src, src_sums, tgt, tgt_sums = bucket_step(
        src_ref[...], src_sums_ref[0], tgt_ref[...], tgt_sums_ref[0], operators[:, :lanes],
        s_ref[0, 0, 0:1, :], d_ref[0, 0, 0:1, :], counts[0], negs,
    )
    store_block(src_out, src, src_sums)
    store_block(tgt_a_out, tgt, tgt_sums)
    store_block(tgt_b_out, tgt, tgt_sums)


def second_kernel(negs, tgt_a_ref, src_ref, moved_ref, tgt_b_ref, own_ref, src_far_out, tgt_a_out, src_out, tgt_b_out):
    row, col = lax.axis_index("row"), lax.axis_index("col")
    width = src_ref.shape[0] - PAD
    tgt = jnp.where(from_late(col, LATE_FIRST), tgt_a_ref[...], tgt_b_ref[...])
    pack = jnp.where(takes_moved(row, col, lax.axis_size("row")), moved_ref[...], own_ref[...])
    src, src_sums, tgt, tgt_sums = bucket_step(
        src_ref[:width, :], src_ref[width : width + 1, :], tgt[:width], tgt[width : width + 1], pack[:width],
        pack[width : width + 1].astype(jnp.int32), pack[width + 1 : width + 2].astype(jnp.int32),
        pack[width + 2 : width + 3], negs,
    )
    store_block(src_far_out, src, src_sums)
    store_block(src_out, src, src_sums)
    store_block(tgt_a_out, tgt, tgt_sums)
    store_block(tgt_b_out, tgt, tgt_sums)


def from_late(col, late):
    return lax.rem(col + RUN - 1, RUN) >= late


def crosses(row, rows):
    return (row + 1) % (rows // 2) == 0


def moves(row, rows):
    return jnp.logical_or(lax.rem(row + 1, rows // 2) == 0, row == rows // 2)


def takes_moved(row, col, rows):
    return jnp.logical_and(lax.rem(col, RUN) == 0, moves(row, rows))


def place(row, col, rows, cols):
    group, z = divmod(col, RUN)
    if z == 0 and (crosses(row, rows) or row == rows // 2):
        group -= 1
    return row, group % (cols // RUN) * RUN + z


def unpack_kernel(src_far_ref, tgt_a_ref, src_ref, tgt_b_ref, src_out, src_sums_out, tgt_out, tgt_sums_out, sems):
    width = src_out.shape[0]

    def send(ref, out, sums_out, first):
        pairs = [(ref.at[pl.ds(0, width)], out), (ref.at[pl.ds(width, 1)], sums_out.at[0])]
        return [pltpu.make_async_copy(a, b, sems.at[first + i]) for i, (a, b) in enumerate(pairs)]

    def move(src_ref, tgt_ref):
        copies = send(src_ref, src_out, src_sums_out, 0) + send(tgt_ref, tgt_out, tgt_sums_out, 2)
        for copy in copies:
            copy.start()
        for copy in copies:
            copy.wait()

    row, col = lax.axis_index("row"), lax.axis_index("col")
    rows = lax.axis_size("row")
    z = lax.rem(col, RUN)
    src_far = jnp.logical_and(z == 0, lax.rem(row, rows // 2) == 0)
    from_moved = jnp.logical_and(z == 1, lax.rem(row + 1, rows // 2) == 0)
    tgt_a = jnp.logical_or(from_late(col, LATE_SECOND), from_moved)
    for far in (False, True):
        for a in (False, True):
            chosen = jnp.logical_and(src_far == far, tgt_a == a)
            refs = (src_far_ref if far else src_ref, tgt_a_ref if a else tgt_b_ref)
            pl.when(chosen)(functools.partial(move, *refs))


def routes(rows, cols):
    def pairs(source, target, keep=lambda r, c: True):
        found = []
        for r in range(rows):
            for c in range(cols):
                (r0, c0), (r1, c1) = source(r, c), target(r, c)
                if keep(r, c):
                    found.append((r0 * cols + c0, r1 * cols + c1))
        return found

    def home(r, c):
        return r, c

    def there(r, c):
        return place(r, c, rows, cols)

    def back_row(r, c):
        return (r - 1) % rows, c

    def back_col(r, c):
        return r, (c - 1) % cols

    def next_row(r, c):
        return (r + 1) % rows, c

    def next_col(r, c):
        return r, (c + 1) % cols

    def late_first(r, c):
        return (c - 1) % RUN >= LATE_FIRST

    def late_second(r, c):
        return c % RUN >= LATE_SECOND or (c % RUN == 0 and crosses(r, rows))

    def wraps_early(r, c):
        return c % RUN == 0 and crosses(r, rows)

    def negate(f):
        return lambda r, c: not f(r, c)

    return {
        "first_tgt_a": pairs(back_col, there, late_first),
        "first_src": pairs(back_row, there),
        "moved": pairs(home, there, lambda r, c: there(r, c) != (r, c)),
        "first_tgt_b": pairs(back_col, there, negate(late_first)),
        "second_tgt_a": pairs(there, next_col, late_second),
        "second_src_far": pairs(there, next_row, wraps_early),
        "second_src": pairs(there, next_row, negate(wraps_early)),
        "second_tgt_b": pairs(there, next_col, negate(late_second)),
    }


def on_device(
    source_emb, source_acc, target_emb, target_acc, relations, src_index, dst_index, rel_index, neg_index
):
    src, tgt = source_emb[0, 0].T, target_emb[0, 0].T
    width, entities = src.shape
    types = relations.shape[0]
    edges, negs = src_index.shape[3], neg_index.shape[3]
    block = pltpu.VMEM((width + PAD, entities), f32)
    route = routes(lax.axis_size("row"), lax.axis_size("col"))

    def send(x, name):
        return lax.ppermute(x, ("row", "col"), route[name])

    vmem = pl.BlockSpec(memory_space=pltpu.VMEM)
    hbm = pl.BlockSpec(memory_space=pltpu.HBM)
    params = pltpu.CompilerParams(vmem_limit_bytes=VMEM_LIMIT)

    operands = (src, source_acc, tgt, target_acc, relations.T, src_index, dst_index, rel_index, neg_index)
    tgt_a, src, moved, tgt_b, own = pl.pallas_call(
        first_kernel,
        name="first_step",
        out_shape=(
            block,
            block,
            block,
            block,
            block,
        ),
        in_specs=[hbm] * len(operands),
        out_specs=(vmem,) * 5,
        scratch_shapes=[pltpu.VMEM(x.shape, x.dtype) for x in operands]
        + [pltpu.VMEM((types, 2 * edges), bf16), pltpu.SemaphoreType.DMA((len(operands) + 1,))],
        compiler_params=params,
    )(*[pltpu.with_memory_space_constraint(x, pltpu.HBM) for x in operands])
    tgt_a = send(tgt_a, "first_tgt_a")
    src = send(src, "first_src")
    moved = send(moved, "moved")
    tgt_b = send(tgt_b, "first_tgt_b")
    src_far, tgt_a, src, tgt_b = pl.pallas_call(
        functools.partial(second_kernel, negs),
        name="second_step",
        out_shape=(block,) * 4,
        in_specs=[vmem] * 5,
        out_specs=(vmem,) * 4,
        compiler_params=params,
    )(tgt_a, src, moved, tgt_b, own)
    src_far = send(src_far, "second_src_far")
    tgt_a = send(tgt_a, "second_tgt_a")
    src = send(src, "second_src")
    tgt_b = send(tgt_b, "second_tgt_b")
    table = pltpu.HBM((width, entities), f32)
    sums = pltpu.HBM((1, 1, entities), f32)
    src, src_sums, tgt, tgt_sums = pl.pallas_call(
        unpack_kernel,
        name="unpack",
        out_shape=(table, sums, table, sums),
        in_specs=[vmem] * 4,
        out_specs=(hbm,) * 4,
        scratch_shapes=[pltpu.SemaphoreType.DMA((4,))],
        compiler_params=params,
    )(src_far, tgt_a, src, tgt_b)
    return src.T[None, None], src_sums, tgt.T[None, None], tgt_sums


def solution(mesh):
    grid4 = P("row", "col", None, None)
    grid3 = P("row", "col", None)
    return jax.shard_map(
        on_device,
        mesh=mesh,
        in_specs=(grid4, grid3, grid4, grid3, P(), grid4, grid4, grid4, grid4),
        out_specs=(grid4, grid3, grid4, grid3),
        check_vma=False,
    )
```

```python
import functools

import jax
import jax.numpy as jnp
from jax import lax
from jax.experimental import pallas as pl
from jax.experimental.pallas import tpu as pltpu
from jax.sharding import PartitionSpec as P


learning_rate = 0.1
bf16 = jnp.bfloat16
f32 = jnp.float32
PAD = 8
CHUNK = 512
RUN = 8
LATE = 5
FINAL_COST = 50
VMEM_LIMIT = 32 * 1024 * 1024

plain = (((1,), (0,)), ((), ()))
left_t = (((0,), (0,)), ((), ()))
right_t = (((1,), (1,)), ((), ()))


def cost(microseconds):
    return pl.CostEstimate(flops=int(microseconds * 1e9), bytes_accessed=0, transcendentals=0)


def mm(a, b, dims=plain):
    return lax.dot_general(a, b, dims, preferred_element_type=f32)


def two_parts(x):
    hi = x.astype(bf16)
    lo = (x - hi.astype(f32)).astype(bf16)
    return hi, lo


def one_hot(index_row, size):
    at = lax.broadcasted_iota(jnp.int32, (size, index_row.shape[1]), 0)
    return jnp.where(at == index_row, 1.0, 0.0).astype(f32)


def count_rows(neg_rows, entities):
    held = one_hot(neg_rows[0], entities)
    for row in neg_rows[1:]:
        held = held + one_hot(row, entities)
    return mm(jnp.ones((8, held.shape[1]), bf16), held.astype(bf16), right_t)[0:1]


def bucket_step(src, src_sums, tgt, tgt_sums, operators, src_rows, dst_rows, counts, negs):
    width, entities = src.shape
    half = width // 2

    pick_s = one_hot(src_rows, entities).astype(bf16)
    pick_d = one_hot(dst_rows, entities).astype(bf16)
    op_re, op_im = operators[:half], operators[half:]
    rows = mm(jnp.concatenate(two_parts(src), axis=1), jnp.concatenate([pick_s, pick_s], axis=0))
    matched = mm(jnp.concatenate(two_parts(tgt), axis=1), jnp.concatenate([pick_d, pick_d], axis=0))
    re, im = rows[:half], rows[half:]
    queries = jnp.concatenate([re * op_re - im * op_im, re * op_im + im * op_re], axis=0)
    positive = jnp.sum(queries * matched, axis=0, keepdims=True)
    pos_grad = -1.0 / (1.0 + jnp.exp(positive))

    queries_b = queries.astype(bf16)
    target_b = tgt.astype(bf16)
    scores = mm(target_b, queries_b, left_t)
    weights = ((1.0 / (1.0 + jnp.exp(-scores))) * (1.0 / negs)).astype(bf16)

    counted = jnp.concatenate(two_parts(target_b.astype(f32) * counts), axis=1)
    pull = mm(counted, jnp.concatenate([weights, weights], axis=0))
    grad = pos_grad * matched + pull
    g_re, g_im = grad[:half], grad[half:]
    back = jnp.concatenate([g_re * op_re + g_im * op_im, g_im * op_re - g_re * op_im], axis=0)
    src_grad = mm(
        jnp.concatenate(two_parts(back), axis=1), jnp.concatenate([pick_s, pick_s], axis=1), right_t
    )

    tgt_grad = mm(queries_b, weights, right_t) * counts + mm(
        jnp.concatenate(two_parts(pos_grad * queries), axis=1),
        jnp.concatenate([pick_d, pick_d], axis=1),
        right_t,
    )

    def adagrad(table, sums, g):
        new_sums = sums + jnp.sum(g * g, axis=0, keepdims=True) * (1.0 / width)
        return table - g * (learning_rate / jnp.sqrt(new_sums)), new_sums

    src, src_sums = adagrad(src, src_sums, src_grad)
    tgt, tgt_sums = adagrad(tgt, tgt_sums, tgt_grad)
    return src, src_sums, tgt, tgt_sums


def store_block(ref, table, sums):
    width = table.shape[0]
    ref[:width, :] = table
    ref[width:, :] = jnp.broadcast_to(sums, (ref.shape[0] - width, sums.shape[1]))


def first_kernel(
    src_hbm, src_sums_hbm, tgt_hbm, tgt_sums_hbm, table_hbm, s_hbm, d_hbm, g_hbm, n_hbm,
    tgt_a_out, src_out, tgt_b_out, tgt_c_out, own_out,
    src_ref, src_sums_ref, tgt_ref, tgt_sums_ref, table_ref, s_ref, d_ref, g_ref, n_ref, pick_ref, sems,
):
    width, entities = src_ref.shape
    types = table_ref.shape[1]
    lanes = s_ref.shape[3]
    cut = (width // 2 + 15) // 16 * 16
    parts = [(0, cut), (cut, width - cut)]
    pairs = [(g_hbm, g_ref)]
    pairs += [(table_hbm.at[pl.ds(a, n)], table_ref.at[pl.ds(a, n)]) for a, n in parts]
    pairs += [
        (src_hbm, src_ref), (tgt_hbm, tgt_ref), (s_hbm, s_ref), (d_hbm, d_ref), (n_hbm, n_ref),
        (src_sums_hbm, src_sums_ref), (tgt_sums_hbm, tgt_sums_ref),
    ]
    copies = [pltpu.make_async_copy(a, b, sems.at[i]) for i, (a, b) in enumerate(pairs)]
    for copy in copies:
        copy.start()
    copies[0].wait()
    wanted = jnp.concatenate([g_ref[0, 0, 0:1, :], g_ref[0, 0, 1:2, :]], axis=1)
    for k in range(0, types, CHUNK):
        n = min(CHUNK, types - k)
        pick_ref[k : k + n, :] = one_hot(wanted - k, n).astype(bf16)
    pieces = []
    for copy, (a, n) in zip(copies[1:3], parts):
        copy.wait()
        pieces.append(mm(table_ref[a : a + n, :], pick_ref[...]))
    for copy in copies[3:]:
        copy.wait()
    operators = jnp.concatenate(pieces, axis=0)
    negs = n_ref.shape[3]
    counts = [
        count_rows([n_ref[0, 0, t : t + 1, k : k + lanes] for k in range(0, negs, lanes)], src_ref.shape[1])
        for t in range(2)
    ]
    index = [s_ref[0, 0, 1:2, :].astype(f32), d_ref[0, 0, 1:2, :].astype(f32), counts[1]]
    index = jnp.concatenate(index + [jnp.zeros((PAD - len(index), lanes), f32)], axis=0)
    own_out[:width, :] = operators[:, lanes:]
    own_out[width:, :] = index
    src, src_sums, tgt, tgt_sums = bucket_step(
        src_ref[...], src_sums_ref[0], tgt_ref[...], tgt_sums_ref[0], operators[:, :lanes],
        s_ref[0, 0, 0:1, :], d_ref[0, 0, 0:1, :], counts[0], negs,
    )
    store_block(src_out, src, src_sums)
    store_block(tgt_a_out, tgt, tgt_sums)
    store_block(tgt_c_out, tgt, tgt_sums)
    store_block(tgt_b_out, tgt, tgt_sums)


def second(negs, tgt, src_ref, own_ref):
    width = src_ref.shape[0] - PAD
    pack = own_ref[...]
    return bucket_step(
        src_ref[:width, :], src_ref[width : width + 1, :], tgt[:width], tgt[width : width + 1], pack[:width],
        pack[width : width + 1].astype(jnp.int32), pack[width + 1 : width + 2].astype(jnp.int32),
        pack[width + 2 : width + 3], negs,
    )


def second_kernel(negs, tgt_a_ref, src_ref, tgt_b_ref, own_ref, tgt_a_out, src_out, tgt_out):
    row, col = lax.axis_index("row"), lax.axis_index("col")

    @pl.when(jnp.logical_not(is_last(row, col, lax.axis_size("row"))))
    def _():
        tgt = jnp.where(from_late(col, LATE), tgt_a_ref[...], tgt_b_ref[...])
        src, src_sums, tgt, tgt_sums = second(negs, tgt, src_ref, own_ref)
        store_block(src_out, src, src_sums)
        store_block(tgt_a_out, tgt, tgt_sums)
        store_block(tgt_out, tgt, tgt_sums)


def last_kernel(negs, done_tgt_ref, tgt_c_ref, src_ref, own_ref, tgt_b_out, src_out):
    last = is_last(lax.axis_index("row"), lax.axis_index("col"), lax.axis_size("row"))

    @pl.when(last)
    def _():
        src, src_sums, tgt, tgt_sums = second(negs, tgt_c_ref[...], src_ref, own_ref)
        store_block(src_out, src, src_sums)
        store_block(tgt_b_out, tgt, tgt_sums)

    @pl.when(jnp.logical_not(last))
    def _():
        tgt_b_out[...] = done_tgt_ref[...]


def from_late(col, late):
    return lax.rem(col + RUN - 1, RUN) >= late


def is_last(row, col, rows):
    return jnp.logical_and(lax.rem(col, RUN) == 0, lax.rem(row, rows // 2) == 0)


def unpack(ref, out, sums_out, sems):
    width = out.shape[0]
    pairs = [(ref.at[pl.ds(0, width)], out), (ref.at[pl.ds(width, 1)], sums_out.at[0])]
    return [pltpu.make_async_copy(a, b, sems.at[i]) for i, (a, b) in enumerate(pairs)]


def run(copies):
    for copy in copies:
        copy.start()
    for copy in copies:
        copy.wait()


def receives(row, col, rows):
    return jnp.logical_not(is_last(row + rows - 1, col, rows)), from_late(col, LATE)


def unpack_kernel(tgt_ref, src_ref, src_out, src_sums_out, tgt_out, tgt_sums_out, src_sems, tgt_sems):
    takes_src, takes_tgt = receives(lax.axis_index("row"), lax.axis_index("col"), lax.axis_size("row"))
    src = lambda: unpack(src_ref, src_out, src_sums_out, src_sems)
    tgt = lambda: unpack(tgt_ref, tgt_out, tgt_sums_out, tgt_sems)
    pl.when(jnp.logical_and(takes_src, takes_tgt))(lambda: run(src() + tgt()))
    pl.when(jnp.logical_and(takes_src, jnp.logical_not(takes_tgt)))(lambda: run(src()))
    pl.when(jnp.logical_and(jnp.logical_not(takes_src), takes_tgt))(lambda: run(tgt()))


def unpack_rest_kernel(
    _0, _1, _2, _3, src_ref, tgt_ref, src_out, src_sums_out, tgt_out, tgt_sums_out, src_sems, tgt_sems
):
    takes_src, takes_tgt = receives(lax.axis_index("row"), lax.axis_index("col"), lax.axis_size("row"))
    pl.when(jnp.logical_not(takes_src))(lambda: run(unpack(src_ref, src_out, src_sums_out, src_sems)))
    pl.when(jnp.logical_not(takes_tgt))(lambda: run(unpack(tgt_ref, tgt_out, tgt_sums_out, tgt_sems)))


def routes(rows, cols):
    def pairs(to, keep):
        found = []
        for r in range(rows):
            for c in range(cols):
                if keep(r, c):
                    r1, c1 = to(r, c)
                    found.append((r * cols + c, r1 * cols + c1))
        return found

    def next_row(r, c):
        return (r + 1) % rows, c

    def next_col(r, c):
        return r, (c + 1) % cols

    def late(r, c):
        return c % RUN >= LATE

    def last(r, c):
        return r % (rows // 2) == 0 and c % RUN == 0

    def to_last(r, c):
        return last(*next_col(r, c))

    return {
        "first_tgt_a": pairs(next_col, lambda r, c: late(r, c) and not to_last(r, c)),
        "first_src": pairs(next_row, lambda r, c: True),
        "first_tgt_b": pairs(next_col, lambda r, c: not late(r, c)),
        "first_tgt_c": pairs(next_col, to_last),
        "second_tgt_a": pairs(next_col, late),
        "second_src": pairs(next_row, lambda r, c: not last(r, c)),
        "second_src_c": pairs(next_row, last),
        "second_tgt_b": pairs(next_col, lambda r, c: not late(r, c)),
    }


def on_device(
    source_emb, source_acc, target_emb, target_acc, relations, src_index, dst_index, rel_index, neg_index
):
    src, tgt = source_emb[0, 0].T, target_emb[0, 0].T
    width, entities = src.shape
    types = relations.shape[0]
    edges, negs = src_index.shape[3], neg_index.shape[3]
    block = pltpu.VMEM((width + PAD, entities), f32)
    route = routes(lax.axis_size("row"), lax.axis_size("col"))

    def send(x, name):
        return lax.ppermute(x, ("row", "col"), route[name])

    vmem = pl.BlockSpec(memory_space=pltpu.VMEM)
    hbm = pl.BlockSpec(memory_space=pltpu.HBM)
    params = pltpu.CompilerParams(vmem_limit_bytes=VMEM_LIMIT)

    operands = (src, source_acc, tgt, target_acc, relations.T, src_index, dst_index, rel_index, neg_index)
    tgt_a, src, tgt_b, tgt_c, own = pl.pallas_call(
        first_kernel,
        name="first_step",
        out_shape=(
            block,
            block,
            block,
            block,
            block,
        ),
        in_specs=[hbm] * len(operands),
        out_specs=(vmem,) * 5,
        scratch_shapes=[pltpu.VMEM(x.shape, x.dtype) for x in operands]
        + [pltpu.VMEM((types, 2 * edges), bf16), pltpu.SemaphoreType.DMA((len(operands) + 1,))],
        compiler_params=params,
    )(*[pltpu.with_memory_space_constraint(x, pltpu.HBM) for x in operands])
    tgt_a = send(tgt_a, "first_tgt_a")
    src = send(src, "first_src")
    tgt_b = send(tgt_b, "first_tgt_b")
    tgt_c = send(tgt_c, "first_tgt_c")
    tgt_a, src_a, tgt = pl.pallas_call(
        functools.partial(second_kernel, negs),
        name="second_step",
        out_shape=(block,) * 3,
        in_specs=[vmem] * 4,
        out_specs=(vmem,) * 3,
        compiler_params=params,
        cost_estimate=cost(0.001),
    )(tgt_a, src, tgt_b, own)
    tgt_a = send(tgt_a, "second_tgt_a")
    src_a = send(src_a, "second_src")
    tgt_b, src_c = pl.pallas_call(
        functools.partial(last_kernel, negs),
        name="last_second_step",
        out_shape=(block,) * 2,
        in_specs=[vmem] * 4,
        out_specs=(vmem,) * 2,
        compiler_params=params,
        cost_estimate=cost(0.001),
    )(tgt, tgt_c, src, own)
    src_c = send(src_c, "second_src_c")
    tgt_b = send(tgt_b, "second_tgt_b")
    table = pltpu.HBM((width, entities), f32)
    sums = pltpu.HBM((1, 1, entities), f32)
    out = pl.pallas_call(
        unpack_kernel,
        name="unpack",
        out_shape=(table, sums, table, sums),
        in_specs=[vmem] * 2,
        out_specs=(hbm,) * 4,
        scratch_shapes=[pltpu.SemaphoreType.DMA((2,))] * 2,
        compiler_params=params,
        cost_estimate=cost(FINAL_COST),
    )(tgt_a, src_a)
    src, src_sums, tgt, tgt_sums = pl.pallas_call(
        unpack_rest_kernel,
        name="unpack_rest",
        out_shape=(table, sums, table, sums),
        in_specs=[hbm] * 4 + [vmem] * 2,
        out_specs=(hbm,) * 4,
        input_output_aliases={i: i for i in range(4)},
        scratch_shapes=[pltpu.SemaphoreType.DMA((2,))] * 2,
        compiler_params=params,
        cost_estimate=cost(FINAL_COST),
    )(*out, src_c, tgt_b)
    return src.T[None, None], src_sums, tgt.T[None, None], tgt_sums


def solution(mesh):
    grid4 = P("row", "col", None, None)
    grid3 = P("row", "col", None)
    return jax.shard_map(
        on_device,
        mesh=mesh,
        in_specs=(grid4, grid3, grid4, grid3, P(), grid4, grid4, grid4, grid4),
        out_specs=(grid4, grid3, grid4, grid3),
        check_vma=False,
    )
```

```python
import functools

import jax
import jax.numpy as jnp
from jax import lax
from jax.experimental import pallas as pl
from jax.experimental.pallas import tpu as pltpu
from jax.sharding import PartitionSpec as P


learning_rate = 0.1
bf16 = jnp.bfloat16
f32 = jnp.float32
PAD = 8
CHUNK = 512
RUN = 8
LATE_FIRST = 6
LATE_SECOND = 7
FINAL_COST = 50
VMEM_LIMIT = 32 * 1024 * 1024

plain = (((1,), (0,)), ((), ()))
left_t = (((0,), (0,)), ((), ()))
right_t = (((1,), (1,)), ((), ()))


def cost(microseconds):
    return pl.CostEstimate(flops=int(microseconds * 1e9), bytes_accessed=0, transcendentals=0)


def mm(a, b, dims=plain):
    return lax.dot_general(a, b, dims, preferred_element_type=f32)


def two_parts(x):
    hi = x.astype(bf16)
    lo = (x - hi.astype(f32)).astype(bf16)
    return hi, lo


def one_hot(index_row, size):
    at = lax.broadcasted_iota(jnp.int32, (size, index_row.shape[1]), 0)
    return jnp.where(at == index_row, 1.0, 0.0).astype(f32)


def count_rows(neg_rows, entities):
    held = one_hot(neg_rows[0], entities)
    for row in neg_rows[1:]:
        held = held + one_hot(row, entities)
    return mm(jnp.ones((8, held.shape[1]), bf16), held.astype(bf16), right_t)[0:1]


def bucket_step(src, src_sums, tgt, tgt_sums, operators, src_rows, dst_rows, counts, negs):
    width, entities = src.shape
    half = width // 2

    pick_s = one_hot(src_rows, entities).astype(bf16)
    pick_d = one_hot(dst_rows, entities).astype(bf16)
    op_re, op_im = operators[:half], operators[half:]
    rows = mm(jnp.concatenate(two_parts(src), axis=1), jnp.concatenate([pick_s, pick_s], axis=0))
    matched = mm(jnp.concatenate(two_parts(tgt), axis=1), jnp.concatenate([pick_d, pick_d], axis=0))
    re, im = rows[:half], rows[half:]
    queries = jnp.concatenate([re * op_re - im * op_im, re * op_im + im * op_re], axis=0)
    positive = jnp.sum(queries * matched, axis=0, keepdims=True)
    pos_grad = -1.0 / (1.0 + jnp.exp(positive))

    queries_b = queries.astype(bf16)
    target_b = tgt.astype(bf16)
    scores = mm(target_b, queries_b, left_t)
    weights = ((1.0 / (1.0 + jnp.exp(-scores))) * (1.0 / negs)).astype(bf16)

    counted = jnp.concatenate(two_parts(target_b.astype(f32) * counts), axis=1)
    pull = mm(counted, jnp.concatenate([weights, weights], axis=0))
    grad = pos_grad * matched + pull
    g_re, g_im = grad[:half], grad[half:]
    back = jnp.concatenate([g_re * op_re + g_im * op_im, g_im * op_re - g_re * op_im], axis=0)
    src_grad = mm(
        jnp.concatenate(two_parts(back), axis=1), jnp.concatenate([pick_s, pick_s], axis=1), right_t
    )

    tgt_grad = mm(queries_b, weights, right_t) * counts + mm(
        jnp.concatenate(two_parts(pos_grad * queries), axis=1),
        jnp.concatenate([pick_d, pick_d], axis=1),
        right_t,
    )

    def adagrad(table, sums, g):
        new_sums = sums + jnp.sum(g * g, axis=0, keepdims=True) * (1.0 / width)
        return table - g * (learning_rate / jnp.sqrt(new_sums)), new_sums

    src, src_sums = adagrad(src, src_sums, src_grad)
    tgt, tgt_sums = adagrad(tgt, tgt_sums, tgt_grad)
    return src, src_sums, tgt, tgt_sums


def store_block(ref, table, sums):
    width = table.shape[0]
    ref[:width, :] = table
    ref[width:, :] = jnp.broadcast_to(sums, (ref.shape[0] - width, sums.shape[1]))


def first_kernel(
    src_hbm, src_sums_hbm, tgt_hbm, tgt_sums_hbm, table_hbm, s_hbm, d_hbm, g_hbm, n_hbm,
    tgt_a_out, src_out, tgt_b_out, tgt_c_out, own_out,
    src_ref, src_sums_ref, tgt_ref, tgt_sums_ref, table_ref, s_ref, d_ref, g_ref, n_ref, pick_ref, sems,
):
    width, entities = src_ref.shape
    types = table_ref.shape[1]
    lanes = s_ref.shape[3]
    cut = (width // 2 + 15) // 16 * 16
    parts = [(0, cut), (cut, width - cut)]
    pairs = [(g_hbm, g_ref)]
    pairs += [(table_hbm.at[pl.ds(a, n)], table_ref.at[pl.ds(a, n)]) for a, n in parts]
    pairs += [
        (src_hbm, src_ref), (tgt_hbm, tgt_ref), (s_hbm, s_ref), (d_hbm, d_ref), (n_hbm, n_ref),
        (src_sums_hbm, src_sums_ref), (tgt_sums_hbm, tgt_sums_ref),
    ]
    copies = [pltpu.make_async_copy(a, b, sems.at[i]) for i, (a, b) in enumerate(pairs)]
    for copy in copies:
        copy.start()
    copies[0].wait()
    wanted = jnp.concatenate([g_ref[0, 0, 0:1, :], g_ref[0, 0, 1:2, :]], axis=1)
    for k in range(0, types, CHUNK):
        n = min(CHUNK, types - k)
        pick_ref[k : k + n, :] = one_hot(wanted - k, n).astype(bf16)
    pieces = []
    for copy, (a, n) in zip(copies[1:3], parts):
        copy.wait()
        pieces.append(mm(table_ref[a : a + n, :], pick_ref[...]))
    for copy in copies[3:]:
        copy.wait()
    operators = jnp.concatenate(pieces, axis=0)
    negs = n_ref.shape[3]
    counts = [
        count_rows([n_ref[0, 0, t : t + 1, k : k + lanes] for k in range(0, negs, lanes)], src_ref.shape[1])
        for t in range(2)
    ]
    index = [s_ref[0, 0, 1:2, :].astype(f32), d_ref[0, 0, 1:2, :].astype(f32), counts[1]]
    index = jnp.concatenate(index + [jnp.zeros((PAD - len(index), lanes), f32)], axis=0)
    own_out[:width, :] = operators[:, lanes:]
    own_out[width:, :] = index
    src, src_sums, tgt, tgt_sums = bucket_step(
        src_ref[...], src_sums_ref[0], tgt_ref[...], tgt_sums_ref[0], operators[:, :lanes],
        s_ref[0, 0, 0:1, :], d_ref[0, 0, 0:1, :], counts[0], negs,
    )
    store_block(src_out, src, src_sums)
    store_block(tgt_a_out, tgt, tgt_sums)
    store_block(tgt_c_out, tgt, tgt_sums)
    store_block(tgt_b_out, tgt, tgt_sums)


def second(negs, tgt, src_ref, own_ref):
    width = src_ref.shape[0] - PAD
    pack = own_ref[...]
    return bucket_step(
        src_ref[:width, :], src_ref[width : width + 1, :], tgt[:width], tgt[width : width + 1], pack[:width],
        pack[width : width + 1].astype(jnp.int32), pack[width + 1 : width + 2].astype(jnp.int32),
        pack[width + 2 : width + 3], negs,
    )


def second_kernel(negs, tgt_a_ref, src_ref, tgt_b_ref, own_ref, tgt_a_out, src_out, tgt_out):
    row, col = lax.axis_index("row"), lax.axis_index("col")

    @pl.when(jnp.logical_not(is_last(row, col, lax.axis_size("row"))))
    def _():
        tgt = jnp.where(from_late(col, LATE_FIRST), tgt_a_ref[...], tgt_b_ref[...])
        src, src_sums, tgt, tgt_sums = second(negs, tgt, src_ref, own_ref)
        store_block(src_out, src, src_sums)
        store_block(tgt_a_out, tgt, tgt_sums)
        store_block(tgt_out, tgt, tgt_sums)


def last_kernel(negs, done_tgt_ref, tgt_c_ref, src_ref, own_ref, tgt_b_out, src_out):
    last = is_last(lax.axis_index("row"), lax.axis_index("col"), lax.axis_size("row"))

    @pl.when(last)
    def _():
        src, src_sums, tgt, tgt_sums = second(negs, tgt_c_ref[...], src_ref, own_ref)
        store_block(src_out, src, src_sums)
        store_block(tgt_b_out, tgt, tgt_sums)

    @pl.when(jnp.logical_not(last))
    def _():
        tgt_b_out[...] = done_tgt_ref[...]


def from_late(col, late):
    return lax.rem(col + RUN - 1, RUN) >= late


def is_last(row, col, rows):
    return jnp.logical_and(lax.rem(col, RUN) == 0, lax.rem(row, rows // 2) == 0)


def unpack(ref, out, sums_out, sems):
    width = out.shape[0]
    pairs = [(ref.at[pl.ds(0, width)], out), (ref.at[pl.ds(width, 1)], sums_out.at[0])]
    return [pltpu.make_async_copy(a, b, sems.at[i]) for i, (a, b) in enumerate(pairs)]


def run(copies):
    for copy in copies:
        copy.start()
    for copy in copies:
        copy.wait()


def receives(row, col, rows):
    return jnp.logical_not(is_last(row + rows - 1, col, rows)), from_late(col, LATE_SECOND)


def unpack_kernel(tgt_ref, src_ref, src_out, src_sums_out, tgt_out, tgt_sums_out, src_sems, tgt_sems):
    takes_src, takes_tgt = receives(lax.axis_index("row"), lax.axis_index("col"), lax.axis_size("row"))
    src = lambda: unpack(src_ref, src_out, src_sums_out, src_sems)
    tgt = lambda: unpack(tgt_ref, tgt_out, tgt_sums_out, tgt_sems)
    pl.when(jnp.logical_and(takes_src, takes_tgt))(lambda: run(src() + tgt()))
    pl.when(jnp.logical_and(takes_src, jnp.logical_not(takes_tgt)))(lambda: run(src()))
    pl.when(jnp.logical_and(jnp.logical_not(takes_src), takes_tgt))(lambda: run(tgt()))


def unpack_rest_kernel(
    _0, _1, _2, _3, src_ref, tgt_ref, src_out, src_sums_out, tgt_out, tgt_sums_out, src_sems, tgt_sems
):
    takes_src, takes_tgt = receives(lax.axis_index("row"), lax.axis_index("col"), lax.axis_size("row"))
    pl.when(jnp.logical_not(takes_src))(lambda: run(unpack(src_ref, src_out, src_sums_out, src_sems)))
    pl.when(jnp.logical_not(takes_tgt))(lambda: run(unpack(tgt_ref, tgt_out, tgt_sums_out, tgt_sems)))


def routes(rows, cols):
    def pairs(to, keep):
        found = []
        for r in range(rows):
            for c in range(cols):
                if keep(r, c):
                    r1, c1 = to(r, c)
                    found.append((r * cols + c, r1 * cols + c1))
        return found

    def next_row(r, c):
        return (r + 1) % rows, c

    def next_col(r, c):
        return r, (c + 1) % cols

    def late_first(r, c):
        return c % RUN >= LATE_FIRST

    def late_second(r, c):
        return c % RUN >= LATE_SECOND

    def last(r, c):
        return r % (rows // 2) == 0 and c % RUN == 0

    def to_last(r, c):
        return last(*next_col(r, c))

    return {
        "first_tgt_a": pairs(next_col, lambda r, c: late_first(r, c) and not to_last(r, c)),
        "first_src": pairs(next_row, lambda r, c: True),
        "first_tgt_b": pairs(next_col, lambda r, c: not late_first(r, c)),
        "first_tgt_c": pairs(next_col, to_last),
        "second_tgt_a": pairs(next_col, late_second),
        "second_src": pairs(next_row, lambda r, c: not last(r, c)),
        "second_src_c": pairs(next_row, last),
        "second_tgt_b": pairs(next_col, lambda r, c: not late_second(r, c)),
    }


def on_device(
    source_emb, source_acc, target_emb, target_acc, relations, src_index, dst_index, rel_index, neg_index
):
    src, tgt = source_emb[0, 0].T, target_emb[0, 0].T
    width, entities = src.shape
    types = relations.shape[0]
    edges, negs = src_index.shape[3], neg_index.shape[3]
    block = pltpu.VMEM((width + PAD, entities), f32)
    route = routes(lax.axis_size("row"), lax.axis_size("col"))

    def send(x, name):
        return lax.ppermute(x, ("row", "col"), route[name])

    vmem = pl.BlockSpec(memory_space=pltpu.VMEM)
    hbm = pl.BlockSpec(memory_space=pltpu.HBM)
    params = pltpu.CompilerParams(vmem_limit_bytes=VMEM_LIMIT)

    operands = (src, source_acc, tgt, target_acc, relations.T, src_index, dst_index, rel_index, neg_index)
    tgt_a, src, tgt_b, tgt_c, own = pl.pallas_call(
        first_kernel,
        name="first_step",
        out_shape=(
            block,
            block,
            block,
            block,
            block,
        ),
        in_specs=[hbm] * len(operands),
        out_specs=(vmem,) * 5,
        scratch_shapes=[pltpu.VMEM(x.shape, x.dtype) for x in operands]
        + [pltpu.VMEM((types, 2 * edges), bf16), pltpu.SemaphoreType.DMA((len(operands) + 1,))],
        compiler_params=params,
    )(*[pltpu.with_memory_space_constraint(x, pltpu.HBM) for x in operands])
    tgt_a = send(tgt_a, "first_tgt_a")
    src = send(src, "first_src")
    tgt_b = send(tgt_b, "first_tgt_b")
    tgt_c = send(tgt_c, "first_tgt_c")
    tgt_a, src_a, tgt = pl.pallas_call(
        functools.partial(second_kernel, negs),
        name="second_step",
        out_shape=(block,) * 3,
        in_specs=[vmem] * 4,
        out_specs=(vmem,) * 3,
        compiler_params=params,
        cost_estimate=cost(0.001),
    )(tgt_a, src, tgt_b, own)
    tgt_a = send(tgt_a, "second_tgt_a")
    src_a = send(src_a, "second_src")
    tgt_b, src_c = pl.pallas_call(
        functools.partial(last_kernel, negs),
        name="last_second_step",
        out_shape=(block,) * 2,
        in_specs=[vmem] * 4,
        out_specs=(vmem,) * 2,
        compiler_params=params,
        cost_estimate=cost(0.001),
    )(tgt, tgt_c, src, own)
    src_c = send(src_c, "second_src_c")
    tgt_b = send(tgt_b, "second_tgt_b")
    table = pltpu.HBM((width, entities), f32)
    sums = pltpu.HBM((1, 1, entities), f32)
    out = pl.pallas_call(
        unpack_kernel,
        name="unpack",
        out_shape=(table, sums, table, sums),
        in_specs=[vmem] * 2,
        out_specs=(hbm,) * 4,
        scratch_shapes=[pltpu.SemaphoreType.DMA((2,))] * 2,
        compiler_params=params,
        cost_estimate=cost(FINAL_COST),
    )(tgt_a, src_a)
    src, src_sums, tgt, tgt_sums = pl.pallas_call(
        unpack_rest_kernel,
        name="unpack_rest",
        out_shape=(table, sums, table, sums),
        in_specs=[hbm] * 4 + [vmem] * 2,
        out_specs=(hbm,) * 4,
        input_output_aliases={i: i for i in range(4)},
        scratch_shapes=[pltpu.SemaphoreType.DMA((2,))] * 2,
        compiler_params=params,
        cost_estimate=cost(FINAL_COST),
    )(*out, src_c, tgt_b)
    return src.T[None, None], src_sums, tgt.T[None, None], tgt_sums


def solution(mesh):
    grid4 = P("row", "col", None, None)
    grid3 = P("row", "col", None)
    return jax.shard_map(
        on_device,
        mesh=mesh,
        in_specs=(grid4, grid3, grid4, grid3, P(), grid4, grid4, grid4, grid4),
        out_specs=(grid4, grid3, grid4, grid3),
        check_vma=False,
    )
```

```python
import functools

import jax
import jax.numpy as jnp
from jax import lax
from jax.experimental import pallas as pl
from jax.experimental.pallas import tpu as pltpu
from jax.sharding import PartitionSpec as P


learning_rate = 0.1
bf16 = jnp.bfloat16
f32 = jnp.float32
PAD = 8
CHUNK = 512
RUN = 8
LATE_FIRST = 6
LATE_SECOND = 7
FINAL_COST = 50
VMEM_LIMIT = 32 * 1024 * 1024

plain = (((1,), (0,)), ((), ()))
left_t = (((0,), (0,)), ((), ()))
right_t = (((1,), (1,)), ((), ()))


def cost(microseconds):
    return pl.CostEstimate(flops=int(microseconds * 1e9), bytes_accessed=0, transcendentals=0)


def mm(a, b, dims=plain):
    return lax.dot_general(a, b, dims, preferred_element_type=f32)


def two_parts(x):
    hi = x.astype(bf16)
    lo = (x - hi.astype(f32)).astype(bf16)
    return hi, lo


def one_hot(index_row, size):
    at = lax.broadcasted_iota(jnp.int32, (size, index_row.shape[1]), 0)
    return jnp.where(at == index_row, 1.0, 0.0).astype(f32)


def count_rows(neg_rows, entities):
    held = one_hot(neg_rows[0], entities)
    for row in neg_rows[1:]:
        held = held + one_hot(row, entities)
    return mm(jnp.ones((8, held.shape[1]), bf16), held.astype(bf16), right_t)[0:1]


def bucket_step(src, src_sums, tgt, tgt_sums, operators, src_rows, dst_rows, counts, negs):
    width, entities = src.shape
    half = width // 2

    pick_s = one_hot(src_rows, entities).astype(bf16)
    pick_d = one_hot(dst_rows, entities).astype(bf16)
    op_re, op_im = operators[:half], operators[half:]
    rows = mm(jnp.concatenate(two_parts(src), axis=1), jnp.concatenate([pick_s, pick_s], axis=0))
    matched = mm(jnp.concatenate(two_parts(tgt), axis=1), jnp.concatenate([pick_d, pick_d], axis=0))
    re, im = rows[:half], rows[half:]
    queries = jnp.concatenate([re * op_re - im * op_im, re * op_im + im * op_re], axis=0)
    positive = jnp.sum(queries * matched, axis=0, keepdims=True)
    pos_grad = -1.0 / (1.0 + jnp.exp(positive))

    queries_b = queries.astype(bf16)
    target_b = tgt.astype(bf16)
    scores = mm(target_b, queries_b, left_t)
    weights = ((1.0 / (1.0 + jnp.exp(-scores))) * (1.0 / negs)).astype(bf16)

    counted = jnp.concatenate(two_parts(target_b.astype(f32) * counts), axis=1)
    pull = mm(counted, jnp.concatenate([weights, weights], axis=0))
    grad = pos_grad * matched + pull
    g_re, g_im = grad[:half], grad[half:]
    back = jnp.concatenate([g_re * op_re + g_im * op_im, g_im * op_re - g_re * op_im], axis=0)
    src_grad = mm(
        jnp.concatenate(two_parts(back), axis=1), jnp.concatenate([pick_s, pick_s], axis=1), right_t
    )

    tgt_grad = mm(queries_b, weights, right_t) * counts + mm(
        jnp.concatenate(two_parts(pos_grad * queries), axis=1),
        jnp.concatenate([pick_d, pick_d], axis=1),
        right_t,
    )

    def adagrad(table, sums, g):
        new_sums = sums + jnp.sum(g * g, axis=0, keepdims=True) * (1.0 / width)
        return table - g * (learning_rate / jnp.sqrt(new_sums)), new_sums

    src, src_sums = adagrad(src, src_sums, src_grad)
    tgt, tgt_sums = adagrad(tgt, tgt_sums, tgt_grad)
    return src, src_sums, tgt, tgt_sums


def store_block(ref, table, sums):
    width = table.shape[0]
    ref[:width, :] = table
    ref[width:, :] = jnp.broadcast_to(sums, (ref.shape[0] - width, sums.shape[1]))


def first_kernel(
    src_hbm, src_sums_hbm, tgt_hbm, tgt_sums_hbm, table_hbm, s_hbm, d_hbm, g_hbm, n_hbm,
    tgt_a_out, src_out, tgt_b_out, tgt_c_out, own_out,
    src_ref, src_sums_ref, tgt_ref, tgt_sums_ref, table_ref, s_ref, d_ref, g_ref, n_ref, pick_ref, sems,
):
    width, entities = src_ref.shape
    types = table_ref.shape[1]
    lanes = s_ref.shape[3]
    cut = (width // 2 + 15) // 16 * 16
    parts = [(0, cut), (cut, width - cut)]
    pairs = [(g_hbm, g_ref)]
    pairs += [(table_hbm.at[pl.ds(a, n)], table_ref.at[pl.ds(a, n)]) for a, n in parts]
    pairs += [
        (src_hbm, src_ref), (tgt_hbm, tgt_ref), (s_hbm, s_ref), (d_hbm, d_ref), (n_hbm, n_ref),
        (src_sums_hbm, src_sums_ref), (tgt_sums_hbm, tgt_sums_ref),
    ]
    copies = [pltpu.make_async_copy(a, b, sems.at[i]) for i, (a, b) in enumerate(pairs)]
    for copy in copies:
        copy.start()
    copies[0].wait()
    wanted = jnp.concatenate([g_ref[0, 0, 0:1, :], g_ref[0, 0, 1:2, :]], axis=1)
    for k in range(0, types, CHUNK):
        n = min(CHUNK, types - k)
        pick_ref[k : k + n, :] = one_hot(wanted - k, n).astype(bf16)
    pieces = []
    for copy, (a, n) in zip(copies[1:3], parts):
        copy.wait()
        pieces.append(mm(table_ref[a : a + n, :], pick_ref[...]))
    for copy in copies[3:]:
        copy.wait()
    operators = jnp.concatenate(pieces, axis=0)
    negs = n_ref.shape[3]
    counts = [
        count_rows([n_ref[0, 0, t : t + 1, k : k + lanes] for k in range(0, negs, lanes)], src_ref.shape[1])
        for t in range(2)
    ]
    index = [s_ref[0, 0, 1:2, :].astype(f32), d_ref[0, 0, 1:2, :].astype(f32), counts[1]]
    index = jnp.concatenate(index + [jnp.zeros((PAD - len(index), lanes), f32)], axis=0)
    own_out[:width, :] = operators[:, lanes:]
    own_out[width:, :] = index
    src, src_sums, tgt, tgt_sums = bucket_step(
        src_ref[...], src_sums_ref[0], tgt_ref[...], tgt_sums_ref[0], operators[:, :lanes],
        s_ref[0, 0, 0:1, :], d_ref[0, 0, 0:1, :], counts[0], negs,
    )
    store_block(src_out, src, src_sums)
    store_block(tgt_a_out, tgt, tgt_sums)
    store_block(tgt_c_out, tgt, tgt_sums)
    store_block(tgt_b_out, tgt, tgt_sums)


def second(negs, tgt, src_ref, own_ref):
    width = src_ref.shape[0] - PAD
    pack = own_ref[...]
    return bucket_step(
        src_ref[:width, :], src_ref[width : width + 1, :], tgt[:width], tgt[width : width + 1], pack[:width],
        pack[width : width + 1].astype(jnp.int32), pack[width + 1 : width + 2].astype(jnp.int32),
        pack[width + 2 : width + 3], negs,
    )


def second_kernel(negs, tgt_a_ref, src_ref, tgt_b_ref, own_ref, tgt_a_out, src_out, tgt_out):
    row, col = lax.axis_index("row"), lax.axis_index("col")

    @pl.when(jnp.logical_not(is_last(row, col, lax.axis_size("row"))))
    def _():
        tgt = jnp.where(from_late(col, LATE_FIRST), tgt_a_ref[...], tgt_b_ref[...])
        src, src_sums, tgt, tgt_sums = second(negs, tgt, src_ref, own_ref)
        store_block(src_out, src, src_sums)
        store_block(tgt_a_out, tgt, tgt_sums)
        store_block(tgt_out, tgt, tgt_sums)


def last_kernel(negs, done_tgt_ref, tgt_c_ref, src_ref, own_ref, tgt_b_out, src_out):
    last = is_last(lax.axis_index("row"), lax.axis_index("col"), lax.axis_size("row"))

    @pl.when(last)
    def _():
        src, src_sums, tgt, tgt_sums = second(negs, tgt_c_ref[...], src_ref, own_ref)
        store_block(src_out, src, src_sums)
        store_block(tgt_b_out, tgt, tgt_sums)

    @pl.when(jnp.logical_not(last))
    def _():
        tgt_b_out[...] = done_tgt_ref[...]


def from_late(col, late):
    return lax.rem(col + RUN - 1, RUN) >= late


def is_last(row, col, rows):
    wrap = jnp.logical_and(lax.rem(col, RUN) == 0, lax.rem(row, rows // 2) == 0)
    return jnp.logical_or(wrap, jnp.logical_and(col == 0, lax.rem(row, 2) == 0))


def unpack(ref, out, sums_out, sems):
    width = out.shape[0]
    pairs = [(ref.at[pl.ds(0, width)], out), (ref.at[pl.ds(width, 1)], sums_out.at[0])]
    return [pltpu.make_async_copy(a, b, sems.at[i]) for i, (a, b) in enumerate(pairs)]


def run(copies):
    for copy in copies:
        copy.start()
    for copy in copies:
        copy.wait()


def receives(row, col, rows):
    return jnp.logical_not(is_last(row + rows - 1, col, rows)), from_late(col, LATE_SECOND)


def unpack_kernel(tgt_ref, src_ref, src_out, src_sums_out, tgt_out, tgt_sums_out, src_sems, tgt_sems):
    takes_src, takes_tgt = receives(lax.axis_index("row"), lax.axis_index("col"), lax.axis_size("row"))
    src = lambda: unpack(src_ref, src_out, src_sums_out, src_sems)
    tgt = lambda: unpack(tgt_ref, tgt_out, tgt_sums_out, tgt_sems)
    pl.when(jnp.logical_and(takes_src, takes_tgt))(lambda: run(src() + tgt()))
    pl.when(jnp.logical_and(takes_src, jnp.logical_not(takes_tgt)))(lambda: run(src()))
    pl.when(jnp.logical_and(jnp.logical_not(takes_src), takes_tgt))(lambda: run(tgt()))


def unpack_src_kernel(_0, _1, src_ref, src_out, src_sums_out, src_sems):
    takes_src, _ = receives(lax.axis_index("row"), lax.axis_index("col"), lax.axis_size("row"))
    pl.when(jnp.logical_not(takes_src))(lambda: run(unpack(src_ref, src_out, src_sums_out, src_sems)))


def unpack_tgt_kernel(_0, _1, tgt_ref, tgt_out, tgt_sums_out, tgt_sems):
    _, takes_tgt = receives(lax.axis_index("row"), lax.axis_index("col"), lax.axis_size("row"))
    pl.when(jnp.logical_not(takes_tgt))(lambda: run(unpack(tgt_ref, tgt_out, tgt_sums_out, tgt_sems)))


def routes(rows, cols):
    def pairs(to, keep):
        found = []
        for r in range(rows):
            for c in range(cols):
                if keep(r, c):
                    r1, c1 = to(r, c)
                    found.append((r * cols + c, r1 * cols + c1))
        return found

    def next_row(r, c):
        return (r + 1) % rows, c

    def next_col(r, c):
        return r, (c + 1) % cols

    def late_first(r, c):
        return c % RUN >= LATE_FIRST

    def late_second(r, c):
        return c % RUN >= LATE_SECOND

    def last(r, c):
        return (r % (rows // 2) == 0 and c % RUN == 0) or (c == 0 and r % 2 == 0)

    def to_last(r, c):
        return last(*next_col(r, c))

    return {
        "first_tgt_a": pairs(next_col, lambda r, c: late_first(r, c) and not to_last(r, c)),
        "first_src": pairs(next_row, lambda r, c: True),
        "first_tgt_b": pairs(next_col, lambda r, c: not late_first(r, c)),
        "first_tgt_c": pairs(next_col, to_last),
        "second_tgt_a": pairs(next_col, late_second),
        "second_src": pairs(next_row, lambda r, c: not last(r, c)),
        "second_src_c": pairs(next_row, last),
        "second_tgt_b": pairs(next_col, lambda r, c: not late_second(r, c)),
    }


def on_device(
    source_emb, source_acc, target_emb, target_acc, relations, src_index, dst_index, rel_index, neg_index
):
    src, tgt = source_emb[0, 0].T, target_emb[0, 0].T
    width, entities = src.shape
    types = relations.shape[0]
    edges, negs = src_index.shape[3], neg_index.shape[3]
    block = pltpu.VMEM((width + PAD, entities), f32)
    route = routes(lax.axis_size("row"), lax.axis_size("col"))

    def send(x, name):
        return lax.ppermute(x, ("row", "col"), route[name])

    vmem = pl.BlockSpec(memory_space=pltpu.VMEM)
    hbm = pl.BlockSpec(memory_space=pltpu.HBM)
    params = pltpu.CompilerParams(vmem_limit_bytes=VMEM_LIMIT)

    operands = (src, source_acc, tgt, target_acc, relations.T, src_index, dst_index, rel_index, neg_index)
    tgt_a, src, tgt_b, tgt_c, own = pl.pallas_call(
        first_kernel,
        name="first_step",
        out_shape=(
            block,
            block,
            block,
            block,
            block,
        ),
        in_specs=[hbm] * len(operands),
        out_specs=(vmem,) * 5,
        scratch_shapes=[pltpu.VMEM(x.shape, x.dtype) for x in operands]
        + [pltpu.VMEM((types, 2 * edges), bf16), pltpu.SemaphoreType.DMA((len(operands) + 1,))],
        compiler_params=params,
    )(*[pltpu.with_memory_space_constraint(x, pltpu.HBM) for x in operands])
    tgt_a = send(tgt_a, "first_tgt_a")
    src = send(src, "first_src")
    tgt_b = send(tgt_b, "first_tgt_b")
    tgt_c = send(tgt_c, "first_tgt_c")
    tgt_a, src_a, tgt = pl.pallas_call(
        functools.partial(second_kernel, negs),
        name="second_step",
        out_shape=(block,) * 3,
        in_specs=[vmem] * 4,
        out_specs=(vmem,) * 3,
        compiler_params=params,
        cost_estimate=cost(0.001),
    )(tgt_a, src, tgt_b, own)
    tgt_a = send(tgt_a, "second_tgt_a")
    src_a = send(src_a, "second_src")
    tgt_b, src_c = pl.pallas_call(
        functools.partial(last_kernel, negs),
        name="last_second_step",
        out_shape=(block,) * 2,
        in_specs=[vmem] * 4,
        out_specs=(vmem,) * 2,
        compiler_params=params,
        cost_estimate=cost(0.001),
    )(tgt, tgt_c, src, own)
    src_c = send(src_c, "second_src_c")
    tgt_b = send(tgt_b, "second_tgt_b")
    table = pltpu.HBM((width, entities), f32)
    sums = pltpu.HBM((1, 1, entities), f32)
    out = pl.pallas_call(
        unpack_kernel,
        name="unpack",
        out_shape=(table, sums, table, sums),
        in_specs=[vmem] * 2,
        out_specs=(hbm,) * 4,
        scratch_shapes=[pltpu.SemaphoreType.DMA((2,))] * 2,
        compiler_params=params,
        cost_estimate=cost(FINAL_COST),
    )(tgt_a, src_a)
    src, src_sums, tgt, tgt_sums = out

    def rest(kernel, aliases, *inputs):
        return pl.pallas_call(
            kernel,
            name=kernel.__name__,
            out_shape=(table, sums),
            in_specs=[hbm] * (len(inputs) - 1) + [vmem],
            out_specs=(hbm,) * 2,
            input_output_aliases=aliases,
            scratch_shapes=[pltpu.SemaphoreType.DMA((2,))],
            compiler_params=params,
            cost_estimate=cost(FINAL_COST),
        )(*inputs)

    src, src_sums = rest(unpack_src_kernel, {0: 0, 1: 1}, src, src_sums, src_c)
    tgt, tgt_sums = rest(unpack_tgt_kernel, {0: 0, 1: 1}, tgt, tgt_sums, tgt_b)
    return src.T[None, None], src_sums, tgt.T[None, None], tgt_sums


def solution(mesh):
    grid4 = P("row", "col", None, None)
    grid3 = P("row", "col", None)
    return jax.shard_map(
        on_device,
        mesh=mesh,
        in_specs=(grid4, grid3, grid4, grid3, P(), grid4, grid4, grid4, grid4),
        out_specs=(grid4, grid3, grid4, grid3),
        check_vma=False,
    )
```
